256 devices in a mesh: dp: 16 (over x, z_hi, core), ctx: 16 (over z_lo, y).
Axes of the slice: x: 4, y: 4, z: 8 (z_hi: 2, z_lo: 4; z = z_hi * 4 + z_lo), core: 2. Of those that a mesh axis runs over, the one named last changes fastest.
Arguments:
- projected: bfloat16 [16, 2048, 12288], P('dp', 'ctx'), may hold values from -6 to 6
- short_weight: float32 [3, 12288], replicated, may hold values from -3.5 to 3.5
- filter_taps: float32 [2048, 4096], P('dp', 'ctx'), may hold values from -2 to 2
- skip_gain: float32 [4096], P('ctx'), may hold values from -4 to 4
- upstream: bfloat16 [16, 2048, 4096], P('dp', 'ctx'), may hold values from -6 to 6
Outputs:
- mixer_out: bfloat16 [16, 2048, 4096], P('dp', 'ctx')
- filter_gradient: float32 [2048, 4096], P('dp', 'ctx')
The draws below stay inside these ranges and needn't reach their ends.
All inputs are finite; a program needn't handle non-finite values.
Results may differ from the reference program's by a relative error of at most 0.0057.
Values may be sent and summed in bfloat16 or wider, within the bound.
A program may use at most 192 MiB of HBM per device.

```python
import math
import jax
import jax.numpy as jnp
from jax import lax

CHANNELS = 4096
SHORT = 3
LENGTH = 2048
SEQS = 16


def draw_filter_taps(key, part):
    key = jax.random.fold_in(key, 11)
    rate_key, noise_key = jax.random.split(key)
    shortest = 30.0
    longest = 2.0 * LENGTH
    spread = jax.random.uniform(rate_key, (1, CHANNELS), jnp.float32)
    decay_len = shortest * (longest / shortest) ** spread
    positions = lax.broadcasted_iota(jnp.float32, (LENGTH, CHANNELS), 0)
    envelope = jnp.sqrt(2.0 / decay_len) * jnp.exp(-positions / decay_len)
    noise_part = jax.random.truncated_normal(noise_key, -4.0, 4.0, (LENGTH, CHANNELS), jnp.float32)
    return noise_part * envelope


def block_levels(stream_key, shape, pieces, smallest, high):
    loudness, own = 1.0, jax.random.fold_in(stream_key, 6)
    for dim, parts in pieces:
        steps = jnp.exp(jax.random.uniform(jax.random.fold_in(own, dim), (parts,), jnp.float32, smallest / len(pieces), high / len(pieces)))
        loudness = loudness * jnp.repeat(steps, shape[dim] // parts).reshape([-1 if axis == dim else 1 for axis in range(len(shape))])
    return loudness


def centred(stream_key, dims, width, most, pieces=(), dtype=jnp.bfloat16):
    result = width * jax.random.normal(stream_key, dims, jnp.float32)
    if pieces:
        result = result * block_levels(stream_key, dims, pieces, -0.22, 0.18)
    return jnp.clip(result, -most, most).astype(dtype)


def setup_inputs(seed: int = 0) -> dict:
    seeds = jax.random.split(jax.random.key(seed), 6)
    projected = centred(seeds[0], (SEQS, LENGTH, 3 * CHANNELS), 1.0, 6.0, ((0, 16), (1, 16)))
    short_weight = centred(seeds[1], (SHORT, 3 * CHANNELS), SHORT ** -0.5, 3.5, (), jnp.float32)
    filter_taps = draw_filter_taps(jax.random.fold_in(seeds[5], 71), 0)
    skip_gain = centred(seeds[3], (CHANNELS,), 1.0, 4.0, ((0, 16),), jnp.float32)
    upstream = centred(seeds[4], (SEQS, LENGTH, CHANNELS), 1.0, 6.0, ((0, 16), (1, 16)))
    return dict(projected=projected, short_weight=short_weight, filter_taps=filter_taps, skip_gain=skip_gain, upstream=upstream)


def short_filter(stream, weights):
    taps_count = weights.shape[0]
    row_count = stream.shape[0]
    extended = jnp.pad(stream.astype(jnp.float32), ((taps_count - 1, 0), (0, 0)))
    running = jnp.zeros(stream.shape, jnp.float32)
    for offset in range(taps_count):
        first_row = taps_count - 1 - offset
        running = running + weights[offset] * extended[first_row:first_row + row_count]
    return running

def reference(projected, short_weight, filter_taps, skip_gain, upstream):
    weights = short_weight.reshape(SHORT, 3, CHANNELS)
    streams = projected.reshape(SEQS, LENGTH, 3, CHANNELS)
    fft_size = 2 * LENGTH
    taps_spec = jnp.fft.rfft(filter_taps, n=fft_size, axis=0)
    grad_scale = 1.0 / math.sqrt(SEQS * LENGTH)

    def one_sequence(running, inputs):
        sequence, cotangent = inputs
        gate_q = short_filter(sequence[:, 0], weights[:, 0])
        keys_conv = short_filter(sequence[:, 1], weights[:, 1])
        values_conv = short_filter(sequence[:, 2], weights[:, 2])
        product = lax.optimization_barrier((keys_conv * values_conv).astype(jnp.bfloat16))
        grad_in = lax.optimization_barrier((cotangent.astype(jnp.float32) * gate_q).astype(jnp.bfloat16))
        prod_spec = jnp.fft.rfft(product.astype(jnp.float32), n=fft_size, axis=0)
        convolved = jnp.fft.irfft(prod_spec * taps_spec, n=fft_size, axis=0)[:LENGTH]
        conv_out = lax.optimization_barrier((convolved + skip_gain * product.astype(jnp.float32)).astype(jnp.bfloat16))
        mixed_seq = (gate_q * conv_out.astype(jnp.float32)).astype(jnp.bfloat16)
        grad_spec = jnp.fft.rfft(grad_in.astype(jnp.float32), n=fft_size, axis=0)
        correlation = jnp.fft.irfft(jnp.conj(prod_spec) * grad_spec, n=fft_size, axis=0)[:LENGTH]
        return (running + correlation, mixed_seq)
    initial = jnp.zeros((LENGTH, CHANNELS), jnp.float32)
    summed, mixer_out = lax.scan(one_sequence, initial, (streams, upstream))
    return (mixer_out, summed * grad_scale)
```

```python
import functools
import math

import jax
import jax.numpy as jnp
import ml_dtypes
import numpy as np
from jax import lax
from jax.experimental import pallas as pl
from jax.experimental.pallas import tpu as pltpu
from jax.sharding import PartitionSpec as P

SHORT = 3
BLOCK = 256
HALF = 128
F32 = jnp.float32
BF16 = jnp.bfloat16


def split_table(table):
    high = table.astype(ml_dtypes.bfloat16)
    low = (table - high.astype(np.float64)).astype(ml_dtypes.bfloat16)
    return high, low


def make_tables():
    size = 2 * BLOCK
    freq = np.concatenate([np.arange(0, BLOCK, 2), np.arange(1, BLOCK, 2)])
    time = np.arange(BLOCK)
    angle = 2.0 * np.pi * ((freq[:, None] * time[None, :]) % size) / size
    real, imag = np.cos(angle), -np.sin(angle)
    imag[0] = np.where(time % 2 == 0, 1.0, -1.0)
    forward = np.concatenate([real, imag], axis=0)
    weight = np.full((size, 1), 2.0 / size)
    weight[0] = weight[BLOCK] = 1.0 / size
    inverse = (forward * weight).T
    return split_table(forward) + split_table(inverse)


def dot(a, b):
    return jnp.dot(a, b, preferred_element_type=F32)


def kernel(
    proj, weights, taps, skip, upstream, fwd_hi, fwd_lo, inv_hi, inv_lo,
    mixed, taps_grad,
    pack, halo_out, halo_in, halo, gate, outgoing, incoming, all_taps, taps_spec, spec, joint,
    conv_own, conv_in, grad, core_out, core_in, x_out, x_in, z_out, z_in,
    halo_sems, taps_send, taps_recv, part_send, part_recv, conv_send, conv_recv, red_send, red_recv,
):
    ctx, dp = lax.axis_index("ctx"), lax.axis_index("dp")
    ranks = 16
    rows = proj.shape[0]
    width = proj.shape[1] // 3
    blocks = ranks * rows // BLOCK
    x, zh, core = dp // 4, (dp // 2) % 2, dp % 2
    z_mate = dp + 2 - 4 * zh
    core_mate = dp + 1 - 2 * core

    def rotated(step):
        z, y = (ctx // 4 + step // 4) % 4, (ctx % 4 + step % 4) % 4
        return z * 4 + y

    def plane_mate(step):
        return ((x + step // 2) % 4) * 4 + zh * 2 + (core + step % 2) % 2

    barrier = pltpu.get_barrier_semaphore()

    def greet(step, _):
        pl.semaphore_signal(barrier, inc=1, device_id={"ctx": rotated(step)})
        return 0

    def greet_plane(step, _):
        pl.semaphore_signal(barrier, inc=1, device_id={"dp": plane_mate(step)})
        return 0

    lax.fori_loop(1, ranks, greet, 0)
    lax.fori_loop(1, 8, greet_plane, 0)
    pl.semaphore_signal(barrier, inc=1, device_id={"dp": z_mate})

    piece = 3 * width // 8
    for seg in range(8):
        tail = proj[rows - 16 : rows, seg * piece : (seg + 1) * piece].astype(F32)
        pack[2 * seg : 2 * seg + 2, :] = tail[14:16]
    halo_out[...] = pack[...].astype(BF16)
    all_taps[dp] = taps[...].astype(BF16)

    pl.semaphore_wait(barrier, ranks - 1 + 8)

    halo_copy = pltpu.make_async_remote_copy(
        src_ref=halo_out, dst_ref=halo_in, send_sem=halo_sems.at[0], recv_sem=halo_sems.at[1],
        device_id={"ctx": (ctx + 1) % ranks},
    )
    halo_copy.start()

    def taps_copy(block, slot, target):
        return pltpu.make_async_remote_copy(
            src_ref=all_taps.at[block], dst_ref=all_taps.at[block],
            send_sem=taps_send.at[slot], recv_sem=taps_recv.at[block], device_id={"dp": target},
        )

    taps_copy(dp, 0, z_mate).start()

    def send_own(step, _):
        taps_copy(dp, step, plane_mate(step)).start()
        return 0

    lax.fori_loop(1, 8, send_own, 0)

    halo_copy.wait_recv()
    pack[...] = jnp.where(ctx > 0, halo_in[...].astype(F32), 0.0)
    for seg in range(8):
        halo[0:2, seg * piece : (seg + 1) * piece] = pack[2 * seg : 2 * seg + 2, :]

    row = lax.broadcasted_iota(jnp.int32, (rows, 2 * HALF), 0)

    def short_filter(stream, first):
        cols = pl.ds(pl.multiple_of(stream * width + first, 2 * HALF), 2 * HALF)
        here = proj[:, cols].astype(F32)
        older, old = halo[0:1, cols], halo[1:2, cols]
        back_one = jnp.where(row == 0, old, pltpu.roll(here, 1, 0))
        back_two = jnp.where(row == 0, older, jnp.where(row == 1, old, pltpu.roll(here, 2, 0)))
        w = weights[:, cols]
        return w[0:1] * here + w[1:2] * back_one + w[2:3] * back_two

    def part_copy(chunk, step):
        return pltpu.make_async_remote_copy(
            src_ref=outgoing.at[chunk, step], dst_ref=incoming.at[chunk, ctx],
            send_sem=part_send.at[chunk, step], recv_sem=part_recv.at[chunk, ctx],
            device_id={"ctx": rotated(step)},
        )

    def make_parts(first):
        gate_q = short_filter(0, first)
        product = (short_filter(1, first) * short_filter(2, first)).astype(BF16)
        cols = pl.ds(pl.multiple_of(first, 2 * HALF), 2 * HALF)
        gate[:, cols] = gate_q
        cotangent = (upstream[:, cols].astype(F32) * gate_q).astype(BF16)
        return [
            jnp.concatenate([product[:, lane : lane + HALF], cotangent[:, lane : lane + HALF]], axis=1)
            for lane in (0, HALF)
        ]

    def send_part(index, _):
        step = ranks - 1 - index
        parts = make_parts(rotated(step) * 2 * HALF)
        outgoing[0, step] = parts[0]
        outgoing[1, step] = parts[1]
        part_copy(0, step).start()
        return 0

    lax.fori_loop(0, ranks - 1, send_part, 0)

    def send_late(index, _):
        part_copy(1, ranks - 1 - index).start()
        return 0

    lax.fori_loop(0, ranks - 1, send_late, 0)
    parts = make_parts(ctx * 2 * HALF)
    incoming[0, ctx] = parts[0]
    incoming[1, ctx] = parts[1]

    taps_copy(z_mate, 0, z_mate).wait_recv()

    def forward_taps(step, _):
        taps_copy(z_mate, 7 + step, plane_mate(step)).start()
        return 0

    lax.fori_loop(1, 8, forward_taps, 0)

    def await_taps(step, _):
        taps_copy(plane_mate(step), 0, z_mate).wait_recv()
        taps_copy(plane_mate(step) + 2 - 4 * zh, 0, z_mate).wait_recv()
        return 0

    lax.fori_loop(1, 8, await_taps, 0)

    def transform(block):
        return dot(fwd_hi[...], block) + dot(fwd_lo[...], block)

    def taps_transform(index, _):
        taps_spec[index] = transform(all_taps[pl.ds(2 * index, 2)].reshape(BLOCK, 2 * HALF))
        return 0

    lax.fori_loop(0, blocks, taps_transform, 0)

    def conv_copy(chunk, target):
        return pltpu.make_async_remote_copy(
            src_ref=conv_own.at[chunk, target], dst_ref=conv_in.at[ctx, chunk],
            send_sem=conv_send.at[chunk, target], recv_sem=conv_recv.at[ctx, chunk],
            device_id={"ctx": target},
        )

    sublane = lax.broadcasted_iota(jnp.int32, (8, HALF), 0)
    scale = 1.0 / math.sqrt(ranks * ranks * rows)

    for chunk in range(2):
        lanes = slice(chunk * HALF, (chunk + 1) * HALF)

        def part_transform(index, _):
            for source in (2 * index, 2 * index + 1):

                @pl.when(source != ctx)
                def _():
                    pltpu.make_async_remote_copy(
                        src_ref=outgoing.at[chunk, 0], dst_ref=incoming.at[chunk, source],
                        send_sem=part_send.at[chunk, 0], recv_sem=part_recv.at[chunk, source],
                        device_id={"ctx": rotated(1)},
                    ).wait_recv()

            spec[index] = transform(incoming[chunk, pl.ds(2 * index, 2)].reshape(BLOCK, 2 * HALF))
            return 0

        lax.fori_loop(0, blocks, part_transform, 0)

        def mix(tile, _):
            real = pl.ds(pl.multiple_of(tile * 8, 8), 8)
            imag = pl.ds(pl.multiple_of(BLOCK + tile * 8, 8), 8)
            sign = jnp.where(tile < BLOCK // 16, 1.0, -1.0)
            ends = (sublane + tile * 8) == 0
            p_r = [spec[b, real, 0:HALF] for b in range(blocks)]
            p_i = [spec[b, imag, 0:HALF] for b in range(blocks)]

            h_r = [taps_spec[b, real, lanes] for b in range(blocks)]
            h_i = [taps_spec[b, imag, lanes] for b in range(blocks)]
            p_s = [p_r[b] + p_i[b] for b in range(blocks)]
            h_s = [h_r[b] + h_i[b] for b in range(blocks)]
            last = None
            for b in range(blocks):
                rr = sum(p_r[i] * h_r[b - i] for i in range(1, b + 1)) + p_r[0] * h_r[b] if b else p_r[0] * h_r[0]
                ii = sum(p_i[i] * h_i[b - i] for i in range(1, b + 1)) + p_i[0] * h_i[b] if b else p_i[0] * h_i[0]
                ss = sum(p_s[i] * h_s[b - i] for i in range(1, b + 1)) + p_s[0] * h_s[b] if b else p_s[0] * h_s[0]
                now = (rr - jnp.where(ends, 0.0, ii), jnp.where(ends, ii, ss - rr - ii))
                if last is None:
                    joint[b, real, 0:HALF], joint[b, imag, 0:HALF] = now
                else:
                    joint[b, real, 0:HALF] = now[0] + sign * last[0]
                    joint[b, imag, 0:HALF] = now[1] + sign * last[1]
                last = now

            g_r = [spec[b, real, HALF : 2 * HALF] for b in range(blocks)]
            g_i = [spec[b, imag, HALF : 2 * HALF] for b in range(blocks)]
            p_d = [p_r[b] - p_i[b] for b in range(blocks)]
            g_s = [g_r[b] + g_i[b] for b in range(blocks)]
            last = None
            for b in reversed(range(blocks)):
                rr = p_r[0] * g_r[b]
                ii = p_i[0] * g_i[b]
                ss = p_d[0] * g_s[b]
                for i in range(1, blocks - b):
                    rr = rr + p_r[i] * g_r[b + i]
                    ii = ii + p_i[i] * g_i[b + i]
                    ss = ss + p_d[i] * g_s[b + i]
                now = (rr + jnp.where(ends, 0.0, ii), jnp.where(ends, ii, ss - rr + ii))
                if last is None:
                    joint[b, real, HALF : 2 * HALF], joint[b, imag, HALF : 2 * HALF] = now
                else:
                    joint[b, real, HALF : 2 * HALF] = now[0] + sign * last[0]
                    joint[b, imag, HALF : 2 * HALF] = now[1] + sign * last[1]
                last = now
            return 0

        lax.fori_loop(0, BLOCK // 8, mix, 0)

        def back(index, _):
            b = (ctx // 2 + blocks // 2 + index) % blocks
            value = joint[b]
            high = value.astype(BF16)
            low = (value - high.astype(F32)).astype(BF16)
            result = dot(inv_hi[...], high) + dot(inv_hi[...], low) + dot(inv_lo[...], high)
            product = incoming[chunk, pl.ds(2 * b, 2), :, 0:HALF].reshape(BLOCK, HALF).astype(F32)
            conv = (result[:, 0:HALF] + skip[:, lanes] * product).astype(BF16)
            conv_own[chunk, pl.ds(2 * b, 2)] = conv.reshape(2, HALF, HALF)
            grad[pl.ds(2 * b, 2), :, lanes] = (result[:, HALF : 2 * HALF] * scale).reshape(2, HALF, HALF)
            for target in (2 * b, 2 * b + 1):

                @pl.when(target != ctx)
                def _():
                    conv_copy(chunk, target).start()

            return 0

        lax.fori_loop(0, blocks, back, 0)

    def reduce_copy(slot, source, target, device):
        return pltpu.make_async_remote_copy(
            src_ref=source, dst_ref=target, send_sem=red_send.at[slot], recv_sem=red_recv.at[slot],
            device_id={"dp": device},
        )

    core_copy = reduce_copy(0, core_out, core_in, core_mate)
    x_copies = [
        reduce_copy(i, x_out.at[i - 1], x_in.at[i - 1], ((x + i) % 4) * 4 + zh * 2 + core) for i in (1, 2, 3)
    ]
    z_copy = reduce_copy(4, z_out, z_in, z_mate)

    def core_part(index, _):
        core_out[index] = grad[2 * index + 1 - core].astype(BF16)
        return 0

    lax.fori_loop(0, 8, core_part, 0)
    core_copy.start()
    core_copy.wait_recv()

    for i in (1, 2, 3):
        to = (x + i) % 4
        for half in (0, 1):
            j = 2 * to + half
            x_out[i - 1, half] = (grad[2 * j + core] + core_in[j].astype(F32)).astype(BF16)
        x_copies[i - 1].start()
    for copy in x_copies:
        copy.wait_recv()

    def x_total(half):
        j = 2 * x + half
        total = grad[2 * j + core] + core_in[j].astype(F32)
        for i in range(3):
            total = total + x_in[i, half].astype(F32)
        return total

    z_out[...] = x_total(1 - zh).astype(BF16)
    z_copy.start()

    def finish(index, _):
        source = rotated(index)
        for chunk in range(2):
            cols = pl.ds(pl.multiple_of((source * 2 + chunk) * HALF, HALF), HALF)

            @pl.when(source != ctx)
            def _():
                pltpu.make_async_remote_copy(
                    src_ref=conv_own.at[chunk, 0], dst_ref=conv_in.at[source, chunk],
                    send_sem=conv_send.at[chunk, 0], recv_sem=conv_recv.at[source, chunk],
                    device_id={"ctx": rotated(1)},
                ).wait_recv()
                mixed[:, cols] = (gate[:, cols] * conv_in[source, chunk].astype(F32)).astype(BF16)

            @pl.when(source == ctx)
            def _():
                mixed[:, cols] = (gate[:, cols] * conv_own[chunk, source].astype(F32)).astype(BF16)

        return 0

    lax.fori_loop(0, ranks, finish, 0)

    z_copy.wait_recv()
    taps_grad[...] = x_total(zh) + z_in[...].astype(F32)

    halo_copy.wait_send()

    def drain_taps(step, _):
        taps_copy(dp, step, z_mate).wait_send()
        return 0

    lax.fori_loop(0, 15, drain_taps, 0)

    def drain_parts(step, _):
        for chunk in range(2):
            part_copy(chunk, step).wait_send()
            conv_copy(chunk, rotated(step)).wait_send()
        return 0

    lax.fori_loop(1, ranks, drain_parts, 0)
    core_copy.wait_send()
    for copy in x_copies:
        copy.wait_send()
    z_copy.wait_send()


def per_device(projected, short_weight, filter_taps, skip_gain, upstream):
    rows, joined = projected.shape[1:]
    width = joined // 3
    ranks = 16
    lanes = 2 * HALF
    blocks = ranks * rows // BLOCK
    tables = [jnp.asarray(t) for t in make_tables()]
    vmem = pl.BlockSpec(memory_space=pltpu.VMEM)
    mixed, taps_grad = pl.pallas_call(
        kernel,
        out_shape=[
            jax.ShapeDtypeStruct((rows, width), BF16),
            jax.ShapeDtypeStruct((rows, lanes), F32),
        ],
        in_specs=[vmem] * 9,
        out_specs=[vmem] * 2,
        scratch_shapes=[
            pltpu.VMEM((16, joined // 8), F32),
            pltpu.VMEM((16, joined // 8), BF16),
            pltpu.VMEM((16, joined // 8), BF16),
            pltpu.VMEM((8, joined), F32),
            pltpu.VMEM((rows, width), F32),
            pltpu.VMEM((2, ranks, rows, lanes), BF16),
            pltpu.VMEM((2, ranks, rows, lanes), BF16),
            pltpu.VMEM((ranks, rows, lanes), BF16),
            pltpu.VMEM((blocks, 2 * BLOCK, lanes), F32),
            pltpu.VMEM((blocks, 2 * BLOCK, lanes), F32),
            pltpu.VMEM((blocks, 2 * BLOCK, lanes), F32),
            pltpu.VMEM((2, ranks, rows, HALF), BF16),
            pltpu.VMEM((ranks, 2, rows, HALF), BF16),
            pltpu.VMEM((ranks, rows, lanes), F32),
            pltpu.VMEM((8, rows, lanes), BF16),
            pltpu.VMEM((8, rows, lanes), BF16),
            pltpu.VMEM((3, 2, rows, lanes), BF16),
            pltpu.VMEM((3, 2, rows, lanes), BF16),
            pltpu.VMEM((rows, lanes), BF16),
            pltpu.VMEM((rows, lanes), BF16),
            pltpu.SemaphoreType.DMA((2,)),
            pltpu.SemaphoreType.DMA((16,)),
            pltpu.SemaphoreType.DMA((16,)),
            pltpu.SemaphoreType.DMA((2, 16)),
            pltpu.SemaphoreType.DMA((2, 16)),
            pltpu.SemaphoreType.DMA((2, 16)),
            pltpu.SemaphoreType.DMA((16, 2)),
            pltpu.SemaphoreType.DMA((5,)),
            pltpu.SemaphoreType.DMA((5,)),
        ],
        compiler_params=pltpu.CompilerParams(
            collective_id=0, has_side_effects=True, vmem_limit_bytes=56 * 2**20
        ),
    )(
        projected.reshape(rows, joined), short_weight, filter_taps, skip_gain.reshape(1, lanes),
        upstream.reshape(rows, width), *tables,
    )
    return (mixed.reshape(1, rows, width), taps_grad)


def solution(mesh):
    in_specs = (P("dp", "ctx", None), P(), P("dp", "ctx"), P("ctx"), P("dp", "ctx", None))
    out_specs = (P("dp", "ctx", None), P("dp", "ctx"))
    return jax.shard_map(
        per_device, mesh=mesh, in_specs=in_specs, out_specs=out_specs, check_vma=False
    )
```

```python
import functools
import math

import jax
import jax.numpy as jnp
import ml_dtypes
import numpy as np
from jax import lax
from jax.experimental import pallas as pl
from jax.experimental.pallas import tpu as pltpu
from jax.sharding import PartitionSpec as P

SHORT = 3
BLOCK = 256
HALF = 128
WINDOW = 5
F32 = jnp.float32
BF16 = jnp.bfloat16


def split_table(table):
    high = table.astype(ml_dtypes.bfloat16)
    low = (table - high.astype(np.float64)).astype(ml_dtypes.bfloat16)
    return high, low


def make_tables():
    size = 2 * BLOCK
    freq = np.concatenate([np.arange(0, BLOCK, 2), np.arange(1, BLOCK, 2)])
    time = np.arange(BLOCK)
    angle = 2.0 * np.pi * ((freq[:, None] * time[None, :]) % size) / size
    real, imag = np.cos(angle), -np.sin(angle)
    imag[0] = np.where(time % 2 == 0, 1.0, -1.0)
    forward = np.concatenate([real, imag], axis=0)
    weight = np.full((size, 1), 2.0 / size)
    weight[0] = weight[BLOCK] = 1.0 / size
    inverse = (forward * weight).T
    return np.stack(split_table(forward)), np.stack(split_table(inverse))


def dot(a, b):
    return jnp.dot(a, b, preferred_element_type=F32)


def kernel(
    window, proj_hbm, weights, taps, skip, upstream_hbm, forward_hbm, inverse_hbm,
    mixed, taps_grad,
    proj, upstream, forward, inverse, tail, pack, halo_out, halo_in, halo, gate, mixed_own,
    outgoing, incoming, all_taps, taps_spec, spec, joint, conv_own, conv_in, grad,
    core_out, core_in, x_out, x_in, z_out, z_in,
    load_sems, table_sems, store_sems, halo_sems, taps_send, taps_recv, head_send, head_recv,
    part_send, part_recv, conv_send, conv_recv, red_send, red_recv,
):
    ctx, dp = lax.axis_index("ctx"), lax.axis_index("dp")
    ranks, side = 16, 4
    rows = proj.shape[0]
    width = proj.shape[1] // 3
    lanes = 2 * HALF
    blocks = ranks * rows // BLOCK
    z, y = ctx // side, ctx % side
    x, zh, core = dp // 4, (dp // 2) % 2, dp % 2
    z_mate = dp + 2 - 4 * zh
    core_mate = dp + 1 - 2 * core

    def target_of(step):
        return ((z + step // side) % side) * side + (y + step % side) % side

    def source_of(step):
        return ((z + side - step // side) % side) * side + (y + side - step % side) % side

    def plane_mate(step):
        return ((x + step // 2) % 4) * 4 + zh * 2 + (core + step % 2) % 2

    barrier = pltpu.get_barrier_semaphore()

    def greet(step, _):
        pl.semaphore_signal(barrier, inc=1, device_id={"ctx": target_of(step)})
        return 0

    def greet_plane(step, _):
        pl.semaphore_signal(barrier, inc=1, device_id={"dp": plane_mate(step)})
        return 0

    lax.fori_loop(1, ranks, greet, 0)
    lax.fori_loop(1, 8, greet_plane, 0)
    pl.semaphore_signal(barrier, inc=1, device_id={"dp": z_mate})

    group = side * lanes

    def loads_of(far):
        first = ((z + far) % side) * group
        copies = []
        for stream in range(3):
            cols = pl.ds(pl.multiple_of(stream * width + first, group), group)
            copies.append(
                pltpu.make_async_copy(proj_hbm.at[:, cols], proj.at[:, cols], load_sems.at[far, stream])
            )
        cols = pl.ds(pl.multiple_of(first, group), group)
        copies.append(
            pltpu.make_async_copy(upstream_hbm.at[:, cols], upstream.at[:, cols], load_sems.at[far, 3])
        )
        return copies

    tail_load = pltpu.make_async_copy(proj_hbm.at[pl.ds(rows - 16, 16)], tail, table_sems.at[0])
    tail_load.start()
    for far in (3, 2, 1, 0):
        for copy in loads_of(far):
            copy.start()
    table_loads = [
        pltpu.make_async_copy(forward_hbm, forward, table_sems.at[1]),
        pltpu.make_async_copy(inverse_hbm, inverse, table_sems.at[2]),
    ]
    for copy in table_loads:
        copy.start()

    all_taps[dp] = taps[...].astype(BF16)
    tail_load.wait()
    piece = 3 * width // 8
    for seg in range(8):
        last = tail[:, seg * piece : (seg + 1) * piece].astype(F32)
        pack[2 * seg : 2 * seg + 2, :] = last[14:16]
    halo_out[...] = pack[...].astype(BF16)

    pl.semaphore_wait(barrier, ranks - 1 + 8)

    halo_copy = pltpu.make_async_remote_copy(
        src_ref=halo_out, dst_ref=halo_in, send_sem=halo_sems.at[0], recv_sem=halo_sems.at[1],
        device_id={"ctx": (ctx + 1) % ranks},
    )
    halo_copy.start()

    def taps_copy(block, slot, target):
        return pltpu.make_async_remote_copy(
            src_ref=all_taps.at[block], dst_ref=all_taps.at[block],
            send_sem=taps_send.at[slot], recv_sem=taps_recv.at[block], device_id={"dp": target},
        )

    taps_copy(dp, 0, z_mate).start()

    def body_copy(step, landing):
        body = pl.ds(16, rows - 16)
        return pltpu.make_async_remote_copy(
            src_ref=outgoing.at[0, step, body], dst_ref=incoming.at[0, landing, body],
            send_sem=part_send.at[0, step], recv_sem=part_recv.at[0, landing],
            device_id={"ctx": target_of(step)},
        )

    def head_copy(step, landing):
        head = pl.ds(0, 16)
        return pltpu.make_async_remote_copy(
            src_ref=outgoing.at[0, step, head], dst_ref=incoming.at[0, landing, head],
            send_sem=head_send.at[step], recv_sem=head_recv.at[landing],
            device_id={"ctx": target_of(step)},
        )

    def late_copy(step, landing):
        return pltpu.make_async_remote_copy(
            src_ref=outgoing.at[1, step], dst_ref=incoming.at[1, landing],
            send_sem=part_send.at[1, step], recv_sem=part_recv.at[1, landing],
            device_id={"ctx": target_of(step)},
        )

    def conv_copy(chunk, target, landing):
        return pltpu.make_async_remote_copy(
            src_ref=conv_own.at[chunk, target], dst_ref=conv_in.at[landing, chunk],
            send_sem=conv_send.at[chunk, target], recv_sem=conv_recv.at[landing, chunk],
            device_id={"ctx": target},
        )

    def columns(first):
        return pl.ds(pl.multiple_of(first, lanes), lanes)

    def filtered(stream, first):
        cols = columns(stream * width + first)
        here = proj[:, cols].astype(F32)
        w = weights[:, cols]
        return w[0:1] * here + w[1:2] * pltpu.roll(here, 1, 0) + w[2:3] * pltpu.roll(here, 2, 0)

    head_row = lax.broadcasted_iota(jnp.int32, (16, lanes), 0)

    def filtered_head(stream, first):
        cols = columns(stream * width + first)
        here = proj[0:16, cols].astype(F32)
        older, old = halo[0:1, cols], halo[1:2, cols]
        back_one = jnp.where(head_row == 0, old, pltpu.roll(here, 1, 0))
        back_two = jnp.where(head_row == 0, older, jnp.where(head_row == 1, old, pltpu.roll(here, 2, 0)))
        w = weights[:, cols]
        return w[0:1] * here + w[1:2] * back_one + w[2:3] * back_two

    def make_parts(step, count, filter_rows):
        first = target_of(step) * lanes
        gate_q = filter_rows(0, first)
        product = (filter_rows(1, first) * filter_rows(2, first)).astype(BF16)
        cols = columns(first)
        gate[0:count, cols] = gate_q
        cotangent = (upstream[0:count, cols].astype(F32) * gate_q).astype(BF16)
        return [
            jnp.concatenate([product[:, lane : lane + HALF], cotangent[:, lane : lane + HALF]], axis=1)
            for lane in (0, HALF)
        ]

    def send_body(index, _):
        step = ranks - 1 - index
        parts = make_parts(step, rows, filtered)
        outgoing[0, step] = parts[0]
        outgoing[1, step] = parts[1]
        body_copy(step, ctx).start()
        return 0

    for far in (3, 2, 1, 0):
        for copy in loads_of(far):
            copy.wait()
        lax.fori_loop((3 - far) * side, min((4 - far) * side, ranks - 1), send_body, 0)
    parts = make_parts(0, rows, filtered)
    incoming[0, ctx] = parts[0]
    incoming[1, ctx] = parts[1]

    def send_own(step, _):
        taps_copy(dp, step, plane_mate(step)).start()
        return 0

    lax.fori_loop(1, 8, send_own, 0)

    halo_copy.wait_recv()
    pack[...] = jnp.where(ctx > 0, halo_in[...].astype(F32), 0.0)
    for seg in range(8):
        halo[0:2, seg * piece : (seg + 1) * piece] = pack[2 * seg : 2 * seg + 2, :]

    def send_head(index, _):
        step = ranks - 1 - index
        parts = make_parts(step, 16, filtered_head)
        outgoing[0, step, 0:16] = parts[0]
        outgoing[1, step, 0:16] = parts[1]
        head_copy(step, ctx).start()
        return 0

    lax.fori_loop(0, ranks - 1, send_head, 0)
    parts = make_parts(0, 16, filtered_head)
    incoming[0, ctx, 0:16] = parts[0]
    incoming[1, ctx, 0:16] = parts[1]

    def send_late(index, _):
        late_copy(ranks - 1 - index, ctx).start()
        return 0

    def await_body(index, _):
        step = ranks - 1 - (index - window)
        body_copy(step, source_of(step)).wait_recv()
        return 0

    def await_and_send(index, _):
        await_body(index, 0)
        return send_late(index, 0)

    lax.fori_loop(0, window, send_late, 0)

    taps_copy(z_mate, 0, z_mate).wait_recv()

    def forward_taps(step, _):
        taps_copy(z_mate, 7 + step, plane_mate(step)).start()
        return 0

    lax.fori_loop(1, 8, forward_taps, 0)

    lax.fori_loop(window, ranks - 1, await_and_send, 0)

    def await_taps(step, _):
        taps_copy(plane_mate(step), 0, z_mate).wait_recv()
        taps_copy(plane_mate(step) + 2 - 4 * zh, 0, z_mate).wait_recv()
        return 0

    lax.fori_loop(1, 8, await_taps, 0)
    for copy in table_loads:
        copy.wait()

    def transform(block):
        return dot(forward[0], block) + dot(forward[1], block)

    def taps_transform(index, _):
        taps_spec[index] = transform(all_taps[pl.ds(2 * index, 2)].reshape(BLOCK, lanes))
        return 0

    lax.fori_loop(0, blocks, taps_transform, 0)
    lax.fori_loop(ranks - 1, ranks - 1 + window, await_body, 0)

    def await_head(step, _):
        head_copy(step, source_of(step)).wait_recv()
        return 0

    lax.fori_loop(1, ranks, await_head, 0)

    sublane = lax.broadcasted_iota(jnp.int32, (8, HALF), 0)
    scale = 1.0 / math.sqrt(ranks * ranks * rows)

    def part_transform(chunk, index):
        spec[index] = transform(incoming[chunk, pl.ds(2 * index, 2)].reshape(BLOCK, lanes))

    def rows_of(tile):
        real = pl.ds(pl.multiple_of(tile * 8, 8), 8)
        imag = pl.ds(pl.multiple_of(BLOCK + tile * 8, 8), 8)
        sign = jnp.where(tile < BLOCK // 16, 1.0, -1.0)
        return real, imag, sign, (sublane + tile * 8) == 0

    def put(b, real, imag, sign, now, last):
        at = slice((b % 2) * HALF, (b % 2 + 1) * HALF)
        if last is not None:
            joint[b // 2, real, at] = now[0] + sign * last[0]
            joint[b // 2, imag, at] = now[1] + sign * last[1]
        else:
            joint[b // 2, real, at], joint[b // 2, imag, at] = now

    def sum_products(pairs):
        total = None
        for a, b in pairs:
            total = a * b if total is None else total + a * b
        return total

    def mix_conv(chunk):
        own = slice(chunk * HALF, (chunk + 1) * HALF)

        def tile_step(tile, _):
            real, imag, sign, ends = rows_of(tile)
            p_r = [spec[b, real, 0:HALF] for b in range(blocks)]
            p_i = [spec[b, imag, 0:HALF] for b in range(blocks)]
            h_r = [taps_spec[b, real, own] for b in range(blocks)]
            h_i = [taps_spec[b, imag, own] for b in range(blocks)]
            p_s = [p_r[b] + p_i[b] for b in range(blocks)]
            h_s = [h_r[b] + h_i[b] for b in range(blocks)]
            last = None
            for b in range(blocks):
                rr = sum_products((p_r[i], h_r[b - i]) for i in range(b + 1))
                ii = sum_products((p_i[i], h_i[b - i]) for i in range(b + 1))
                ss = sum_products((p_s[i], h_s[b - i]) for i in range(b + 1))
                now = (rr - jnp.where(ends, 0.0, ii), jnp.where(ends, ii, ss - rr - ii))
                put(b, real, imag, sign, now, last)
                last = now
            return 0

        lax.fori_loop(0, BLOCK // 8, tile_step, 0)

    def mix_grad():
        def tile_step(tile, _):
            real, imag, sign, ends = rows_of(tile)
            p_r = [spec[b, real, 0:HALF] for b in range(blocks)]
            p_i = [spec[b, imag, 0:HALF] for b in range(blocks)]
            g_r = [spec[b, real, HALF:lanes] for b in range(blocks)]
            g_i = [spec[b, imag, HALF:lanes] for b in range(blocks)]
            p_d = [p_r[b] - p_i[b] for b in range(blocks)]
            g_s = [g_r[b] + g_i[b] for b in range(blocks)]
            last = None
            for b in reversed(range(blocks)):
                rr = sum_products((p_r[i], g_r[b + i]) for i in range(blocks - b))
                ii = sum_products((p_i[i], g_i[b + i]) for i in range(blocks - b))
                ss = sum_products((p_d[i], g_s[b + i]) for i in range(blocks - b))
                now = (rr + jnp.where(ends, 0.0, ii), jnp.where(ends, ii, ss - rr + ii))
                put(b, real, imag, sign, now, last)
                last = now
            return 0

        lax.fori_loop(0, BLOCK // 8, tile_step, 0)

    def back(pair):
        value = joint[pair]
        high = value.astype(BF16)
        low = (value - high.astype(F32)).astype(BF16)
        return dot(inverse[0], high) + dot(inverse[0], low) + dot(inverse[1], high)

    def back_conv(chunk, send):
        own = slice(chunk * HALF, (chunk + 1) * HALF)

        def pair_step(index, _):
            pair = (z + side - 1 - index) % side
            result = back(pair)
            for part in range(4):
                target = 4 * pair + part
                value = result[(part % 2) * HALF : (part % 2 + 1) * HALF, (part // 2) * HALF : (part // 2 + 1) * HALF]
                product = incoming[chunk, target, :, 0:HALF].astype(F32)
                conv_own[chunk, target] = (value + skip[:, own] * product).astype(BF16)
                if send:

                    @pl.when(target != ctx)
                    def _():
                        conv_copy(chunk, target, ctx).start()

            return 0

        lax.fori_loop(0, side, pair_step, 0)

    def back_grad(chunk):
        def pair_step(pair, _):
            result = back(pair)
            for part in range(4):
                value = result[(part % 2) * HALF : (part % 2 + 1) * HALF, (part // 2) * HALF : (part // 2 + 1) * HALF]
                grad[chunk, 4 * pair + part] = value * scale
            return 0

        lax.fori_loop(0, side, pair_step, 0)

    def reduce_copy(chunk, slot, source, target, device):
        return pltpu.make_async_remote_copy(
            src_ref=source, dst_ref=target, send_sem=red_send.at[chunk, slot],
            recv_sem=red_recv.at[chunk, slot], device_id={"dp": device},
        )

    def core_copy(chunk):
        return reduce_copy(chunk, 0, core_out.at[chunk], core_in.at[chunk], core_mate)

    def x_copy(chunk, i):
        device = ((x + i) % 4) * 4 + zh * 2 + core
        return reduce_copy(chunk, i, x_out.at[chunk, i - 1], x_in.at[chunk, i - 1], device)

    def z_copy(chunk):
        return reduce_copy(chunk, 4, z_out.at[chunk], z_in.at[chunk], z_mate)

    def core_stage(chunk):
        def part_step(index, _):
            core_out[chunk, index] = grad[chunk, 2 * index + 1 - core].astype(BF16)
            return 0

        lax.fori_loop(0, 8, part_step, 0)
        core_copy(chunk).start()

    def x_stage(chunk):
        core_copy(chunk).wait_recv()
        for i in (1, 2, 3):
            for half in (0, 1):
                j = 2 * ((x + i) % 4) + half
                x_out[chunk, i - 1, half] = (
                    grad[chunk, 2 * j + core] + core_in[chunk, j].astype(F32)
                ).astype(BF16)
            x_copy(chunk, i).start()

    def x_total(chunk, half):
        j = 2 * x + half
        total = grad[chunk, 2 * j + core] + core_in[chunk, j].astype(F32)
        for i in range(3):
            total = total + x_in[chunk, i, half].astype(F32)
        return total

    def z_stage(chunk):
        for i in (1, 2, 3):
            x_copy(chunk, i).wait_recv()
        z_out[chunk] = x_total(chunk, 1 - zh).astype(BF16)
        z_copy(chunk).start()

    def z_finish(chunk):
        z_copy(chunk).wait_recv()
        taps_grad[:, chunk * HALF : (chunk + 1) * HALF] = x_total(chunk, zh) + z_in[chunk].astype(F32)

    def first_transform(index, _):
        part_transform(0, index)
        return 0

    lax.fori_loop(0, blocks, first_transform, 0)
    mix_conv(0)
    back_conv(0, False)
    mix_grad()
    back_grad(0)
    core_stage(0)

    for far in (3, 2, 1, 0):

        def await_late(index, _):
            step = ranks - 1 - index
            late_copy(step, source_of(step)).wait_recv()
            conv_copy(0, target_of(step), ctx).start()
            return 0

        lax.fori_loop((3 - far) * side, min((4 - far) * side, ranks - 1), await_late, 0)
        from_z = (z + side - far) % side
        part_transform(1, 2 * from_z)
        part_transform(1, 2 * from_z + 1)

    x_stage(0)
    mix_conv(1)
    back_conv(1, True)
    z_stage(0)
    mix_grad()
    back_grad(1)
    core_stage(1)

    def gate_part(chunk, source, value):
        cols = pl.ds(pl.multiple_of((source * 2 + chunk) * HALF, HALF), HALF)
        mixed_own[:, cols] = (gate[:, cols] * value.astype(F32)).astype(BF16)

    def gate_step(chunk):
        def one(index, _):
            step = ranks - 1 - index
            source = source_of(step)
            conv_copy(chunk, target_of(1), source).wait_recv()
            gate_part(chunk, source, conv_in[source, chunk])
            return 0

        return one

    gate_part(0, ctx, conv_own[0, ctx])
    gate_part(1, ctx, conv_own[1, ctx])
    x_stage(1)
    lax.fori_loop(0, ranks - 1, gate_step(0), 0)
    z_stage(1)
    z_finish(0)
    stores = []
    for far in (3, 2, 1, 0):
        lax.fori_loop((3 - far) * side, min((4 - far) * side, ranks - 1), gate_step(1), 0)
        cols = pl.ds(pl.multiple_of(((z + side - far) % side) * group, group), group)
        stores.append(pltpu.make_async_copy(mixed_own.at[:, cols], mixed.at[:, cols], store_sems.at[far]))
        stores[-1].start()
    z_finish(1)

    halo_copy.wait_send()

    def drain_taps(step, _):
        taps_copy(dp, step, z_mate).wait_send()
        return 0

    lax.fori_loop(0, 15, drain_taps, 0)

    def drain_parts(step, _):
        body_copy(step, ctx).wait_send()
        head_copy(step, ctx).wait_send()
        late_copy(step, ctx).wait_send()
        for chunk in range(2):
            conv_copy(chunk, target_of(step), ctx).wait_send()
        return 0

    lax.fori_loop(1, ranks, drain_parts, 0)
    for chunk in range(2):
        core_copy(chunk).wait_send()
        for i in (1, 2, 3):
            x_copy(chunk, i).wait_send()
        z_copy(chunk).wait_send()
    for copy in stores:
        copy.wait()


def hand_over(mixed_in, grad_in, mixed, taps_grad, mixed_held, grad_held, load_sems, store_sems):
    parts = 4
    rows = mixed.shape[0] // parts
    loads = [pltpu.make_async_copy(grad_in, grad_held, load_sems.at[parts])]
    stores = [pltpu.make_async_copy(grad_held, taps_grad, store_sems.at[parts])]
    for part in range(parts):
        own = pl.ds(part * rows, rows)
        loads.append(pltpu.make_async_copy(mixed_in.at[own], mixed_held.at[own], load_sems.at[part]))
        stores.append(pltpu.make_async_copy(mixed_held.at[own], mixed.at[own], store_sems.at[part]))
    for load in loads:
        load.start()
    for load, store in zip(loads, stores):
        load.wait()
        store.start()
    for store in stores:
        store.wait()


def per_device(projected, short_weight, filter_taps, skip_gain, upstream):
    rows, joined = projected.shape[1:]
    width = joined // 3
    ranks = 16
    lanes = 2 * HALF
    blocks = ranks * rows // BLOCK
    forward, inverse = (jnp.asarray(t) for t in make_tables())
    vmem = pl.BlockSpec(memory_space=pltpu.VMEM)
    anywhere = pl.BlockSpec(memory_space=pl.ANY)
    shapes = [
        jax.ShapeDtypeStruct((rows, width), BF16),
        jax.ShapeDtypeStruct((rows, lanes), F32),
    ]
    results = pl.pallas_call(
        functools.partial(kernel, WINDOW),
        out_shape=shapes,
        in_specs=[anywhere, vmem, vmem, vmem, anywhere, anywhere, anywhere],
        out_specs=[anywhere, vmem],
        scratch_shapes=[
            pltpu.VMEM((rows, joined), BF16),
            pltpu.VMEM((rows, width), BF16),
            pltpu.VMEM(forward.shape, BF16),
            pltpu.VMEM(inverse.shape, BF16),
            pltpu.VMEM((16, joined), BF16),
            pltpu.VMEM((16, joined // 8), F32),
            pltpu.VMEM((16, joined // 8), BF16),
            pltpu.VMEM((16, joined // 8), BF16),
            pltpu.VMEM((8, joined), F32),
            pltpu.VMEM((rows, width), F32),
            pltpu.VMEM((rows, width), BF16),
            pltpu.VMEM((2, ranks, rows, lanes), BF16),
            pltpu.VMEM((2, ranks, rows, lanes), BF16),
            pltpu.VMEM((ranks, rows, lanes), BF16),
            pltpu.VMEM((blocks, 2 * BLOCK, lanes), F32),
            pltpu.VMEM((blocks, 2 * BLOCK, lanes), F32),
            pltpu.VMEM((blocks // 2, 2 * BLOCK, lanes), F32),
            pltpu.VMEM((2, ranks, rows, HALF), BF16),
            pltpu.VMEM((ranks, 2, rows, HALF), BF16),
            pltpu.VMEM((2, ranks, rows, HALF), F32),
            pltpu.VMEM((2, 8, rows, HALF), BF16),
            pltpu.VMEM((2, 8, rows, HALF), BF16),
            pltpu.VMEM((2, 3, 2, rows, HALF), BF16),
            pltpu.VMEM((2, 3, 2, rows, HALF), BF16),
            pltpu.VMEM((2, rows, HALF), BF16),
            pltpu.VMEM((2, rows, HALF), BF16),
            pltpu.SemaphoreType.DMA((4, 4)),
            pltpu.SemaphoreType.DMA((3,)),
            pltpu.SemaphoreType.DMA((4,)),
            pltpu.SemaphoreType.DMA((2,)),
            pltpu.SemaphoreType.DMA((16,)),
            pltpu.SemaphoreType.DMA((16,)),
            pltpu.SemaphoreType.DMA((16,)),
            pltpu.SemaphoreType.DMA((16,)),
            pltpu.SemaphoreType.DMA((2, 16)),
            pltpu.SemaphoreType.DMA((2, 16)),
            pltpu.SemaphoreType.DMA((2, 16)),
            pltpu.SemaphoreType.DMA((16, 2)),
            pltpu.SemaphoreType.DMA((2, 5)),
            pltpu.SemaphoreType.DMA((2, 5)),
        ],
        compiler_params=pltpu.CompilerParams(
            collective_id=0, has_side_effects=True, vmem_limit_bytes=60 * 2**20
        ),
    )(
        projected.reshape(rows, joined), short_weight, filter_taps, skip_gain.reshape(1, lanes),
        upstream.reshape(rows, width), forward, inverse,
    )
    mixed, taps_grad = pl.pallas_call(
        hand_over,
        out_shape=shapes,
        in_specs=[anywhere] * 2,
        out_specs=[anywhere] * 2,
        scratch_shapes=[
            pltpu.VMEM(shapes[0].shape, BF16),
            pltpu.VMEM(shapes[1].shape, F32),
            pltpu.SemaphoreType.DMA((5,)),
            pltpu.SemaphoreType.DMA((5,)),
        ],
        compiler_params=pltpu.CompilerParams(vmem_limit_bytes=60 * 2**20),
    )(*results)
    return (mixed.reshape(1, rows, width), taps_grad)


def solution(mesh):
    in_specs = (P("dp", "ctx", None), P(), P("dp", "ctx"), P("ctx"), P("dp", "ctx", None))
    out_specs = (P("dp", "ctx", None), P("dp", "ctx"))
    return jax.shard_map(
        per_device, mesh=mesh, in_specs=in_specs, out_specs=out_specs, check_vma=False
    )
```

```python
import functools
import math

import jax
import jax.numpy as jnp
import ml_dtypes
import numpy as np
from jax import lax
from jax.experimental import pallas as pl
from jax.experimental.pallas import tpu as pltpu
from jax.sharding import PartitionSpec as P

SHORT = 3
BLOCK = 256
HALF = 128
WINDOW = 5
F32 = jnp.float32
BF16 = jnp.bfloat16


def split_table(table):
    high = table.astype(ml_dtypes.bfloat16)
    low = (table - high.astype(np.float64)).astype(ml_dtypes.bfloat16)
    return high, low


def make_tables():
    size = 2 * BLOCK
    freq = np.concatenate([np.arange(0, BLOCK, 2), np.arange(1, BLOCK, 2)])
    time = np.arange(BLOCK)
    angle = 2.0 * np.pi * ((freq[:, None] * time[None, :]) % size) / size
    real, imag = np.cos(angle), -np.sin(angle)
    imag[0] = np.where(time % 2 == 0, 1.0, -1.0)
    forward = np.concatenate([real, imag], axis=0)
    weight = np.full((size, 1), 2.0 / size)
    weight[0] = weight[BLOCK] = 1.0 / size
    inverse = (forward * weight).T
    return np.stack(split_table(forward)), np.stack(split_table(inverse))


def dot(a, b):
    return jnp.dot(a, b, preferred_element_type=F32)


def kernel(
    window, proj_hbm, weights_hbm, taps_hbm, skip_hbm, upstream_hbm, forward_hbm, inverse_hbm,
    mixed, taps_grad,
    proj, upstream, weights, taps, skip, forward, inverse, tail, pack, halo_out, halo_in, halo, gate,
    outgoing, incoming, all_taps, taps_spec, spec, joint, conv_own, conv_in, grad,
    core_out, core_in, x_out, x_in, z_out, z_in,
    load_sems, table_sems, halo_sems, taps_send, taps_recv, head_send, head_recv,
    part_send, part_recv, conv_send, conv_recv, red_send, red_recv,
):
    ctx, dp = lax.axis_index("ctx"), lax.axis_index("dp")
    ranks, side = 16, 4
    rows = proj.shape[0]
    width = proj.shape[1] // 3
    lanes = 2 * HALF
    blocks = ranks * rows // BLOCK
    z, y = ctx // side, ctx % side
    x, zh, core = dp // 4, (dp // 2) % 2, dp % 2
    z_mate = dp + 2 - 4 * zh
    core_mate = dp + 1 - 2 * core

    def target_of(step):
        return ((z + step // side) % side) * side + (y + step % side) % side

    def source_of(step):
        return ((z + side - step // side) % side) * side + (y + side - step % side) % side

    def plane_mate(step):
        return ((x + step // 2) % 4) * 4 + zh * 2 + (core + step % 2) % 2

    barrier = pltpu.get_barrier_semaphore()

    def greet(step, _):
        pl.semaphore_signal(barrier, inc=1, device_id={"ctx": target_of(step)})
        return 0

    def greet_plane(step, _):
        pl.semaphore_signal(barrier, inc=1, device_id={"dp": plane_mate(step)})
        return 0

    lax.fori_loop(1, ranks, greet, 0)
    lax.fori_loop(1, 8, greet_plane, 0)
    pl.semaphore_signal(barrier, inc=1, device_id={"dp": z_mate})

    group = side * lanes

    def loads_of(far):
        first = ((z + far) % side) * group
        copies = []
        for stream in range(3):
            cols = pl.ds(pl.multiple_of(stream * width + first, group), group)
            copies.append(
                pltpu.make_async_copy(proj_hbm.at[:, cols], proj.at[:, cols], load_sems.at[far, stream])
            )
        cols = pl.ds(pl.multiple_of(first, group), group)
        copies.append(
            pltpu.make_async_copy(upstream_hbm.at[:, cols], upstream.at[:, cols], load_sems.at[far, 3])
        )
        return copies

    weights_load = pltpu.make_async_copy(weights_hbm, weights, table_sems.at[3])
    weights_load.start()
    for copy in loads_of(3):
        copy.start()
    tail_load = pltpu.make_async_copy(proj_hbm.at[pl.ds(rows - 16, 16)], tail, table_sems.at[0])
    tail_load.start()
    taps_load = pltpu.make_async_copy(taps_hbm, taps, table_sems.at[4])
    taps_load.start()
    for far in (2, 1, 0):
        for copy in loads_of(far):
            copy.start()
    table_loads = [
        pltpu.make_async_copy(forward_hbm, forward, table_sems.at[1]),
        pltpu.make_async_copy(inverse_hbm, inverse, table_sems.at[2]),
        pltpu.make_async_copy(skip_hbm, skip, table_sems.at[5]),
    ]
    for copy in table_loads:
        copy.start()

    weights_load.wait()
    pl.semaphore_wait(barrier, ranks - 1 + 8)

    halo_copy = pltpu.make_async_remote_copy(
        src_ref=halo_out, dst_ref=halo_in, send_sem=halo_sems.at[0], recv_sem=halo_sems.at[1],
        device_id={"ctx": (ctx + 1) % ranks},
    )

    def taps_copy(block, slot, target):
        return pltpu.make_async_remote_copy(
            src_ref=all_taps.at[block], dst_ref=all_taps.at[block],
            send_sem=taps_send.at[slot], recv_sem=taps_recv.at[block], device_id={"dp": target},
        )

    def body_copy(step, landing):
        body = pl.ds(16, rows - 16)
        return pltpu.make_async_remote_copy(
            src_ref=outgoing.at[0, step, body], dst_ref=incoming.at[0, landing, body],
            send_sem=part_send.at[0, step], recv_sem=part_recv.at[0, landing],
            device_id={"ctx": target_of(step)},
        )

    def head_copy(step, landing):
        head = pl.ds(0, 16)
        return pltpu.make_async_remote_copy(
            src_ref=outgoing.at[0, step, head], dst_ref=incoming.at[0, landing, head],
            send_sem=head_send.at[step], recv_sem=head_recv.at[landing],
            device_id={"ctx": target_of(step)},
        )

    def late_copy(step, landing):
        return pltpu.make_async_remote_copy(
            src_ref=outgoing.at[1, step], dst_ref=incoming.at[1, landing],
            send_sem=part_send.at[1, step], recv_sem=part_recv.at[1, landing],
            device_id={"ctx": target_of(step)},
        )

    def conv_copy(chunk, target, landing):
        return pltpu.make_async_remote_copy(
            src_ref=conv_own.at[chunk, target], dst_ref=conv_in.at[landing, chunk],
            send_sem=conv_send.at[chunk, target], recv_sem=conv_recv.at[landing, chunk],
            device_id={"ctx": target},
        )

    def columns(first):
        return pl.ds(pl.multiple_of(first, lanes), lanes)

    def filtered(stream, first):
        cols = columns(stream * width + first)
        here = proj[:, cols].astype(F32)
        w = weights[:, cols]
        return w[0:1] * here + w[1:2] * pltpu.roll(here, 1, 0) + w[2:3] * pltpu.roll(here, 2, 0)

    head_row = lax.broadcasted_iota(jnp.int32, (16, lanes), 0)

    def filtered_head(stream, first):
        cols = columns(stream * width + first)
        here = proj[0:16, cols].astype(F32)
        older, old = halo[0:1, cols], halo[1:2, cols]
        back_one = jnp.where(head_row == 0, old, pltpu.roll(here, 1, 0))
        back_two = jnp.where(head_row == 0, older, jnp.where(head_row == 1, old, pltpu.roll(here, 2, 0)))
        w = weights[:, cols]
        return w[0:1] * here + w[1:2] * back_one + w[2:3] * back_two

    def make_parts(step, count, filter_rows):
        first = target_of(step) * lanes
        gate_q = filter_rows(0, first)
        product = (filter_rows(1, first) * filter_rows(2, first)).astype(BF16)
        cols = columns(first)
        gate[0:count, cols] = gate_q
        cotangent = (upstream[0:count, cols].astype(F32) * gate_q).astype(BF16)
        return [
            jnp.concatenate([product[:, lane : lane + HALF], cotangent[:, lane : lane + HALF]], axis=1)
            for lane in (0, HALF)
        ]

    def send_body(index, _):
        step = ranks - 1 - index
        parts = make_parts(step, rows, filtered)
        outgoing[0, step] = parts[0]
        outgoing[1, step] = parts[1]
        body_copy(step, ctx).start()
        return 0

    piece = 3 * width // 8
    for far in (3, 2, 1, 0):
        for copy in loads_of(far):
            copy.wait()
        lax.fori_loop((3 - far) * side, min((4 - far) * side, ranks - 1), send_body, 0)
        if far == 3:
            tail_load.wait()
            for seg in range(8):
                last = tail[:, seg * piece : (seg + 1) * piece].astype(F32)
                pack[2 * seg : 2 * seg + 2, :] = last[14:16]
            halo_out[...] = pack[...].astype(BF16)
            halo_copy.start()
            taps_load.wait()
            all_taps[dp] = taps[...].astype(BF16)
            taps_copy(dp, 0, z_mate).start()
    parts = make_parts(0, rows, filtered)
    incoming[0, ctx] = parts[0]
    incoming[1, ctx] = parts[1]

    def send_own(step, _):
        taps_copy(dp, step, plane_mate(step)).start()
        return 0

    lax.fori_loop(1, 8, send_own, 0)

    halo_copy.wait_recv()
    pack[...] = jnp.where(ctx > 0, halo_in[...].astype(F32), 0.0)
    for seg in range(8):
        halo[0:2, seg * piece : (seg + 1) * piece] = pack[2 * seg : 2 * seg + 2, :]

    def send_head(index, _):
        step = ranks - 1 - index
        parts = make_parts(step, 16, filtered_head)
        outgoing[0, step, 0:16] = parts[0]
        outgoing[1, step, 0:16] = parts[1]
        head_copy(step, ctx).start()
        return 0

    lax.fori_loop(0, ranks - 1, send_head, 0)
    parts = make_parts(0, 16, filtered_head)
    incoming[0, ctx, 0:16] = parts[0]
    incoming[1, ctx, 0:16] = parts[1]

    def send_late(index, _):
        late_copy(ranks - 1 - index, ctx).start()
        return 0

    def await_body(index, _):
        step = ranks - 1 - (index - window)
        body_copy(step, source_of(step)).wait_recv()
        return 0

    def await_and_send(index, _):
        await_body(index, 0)
        return send_late(index, 0)

    lax.fori_loop(0, window, send_late, 0)

    taps_copy(z_mate, 0, z_mate).wait_recv()

    def forward_taps(step, _):
        taps_copy(z_mate, 7 + step, plane_mate(step)).start()
        return 0

    lax.fori_loop(1, 8, forward_taps, 0)

    lax.fori_loop(window, ranks - 1, await_and_send, 0)

    def await_taps(step, _):
        taps_copy(plane_mate(step), 0, z_mate).wait_recv()
        taps_copy(plane_mate(step) + 2 - 4 * zh, 0, z_mate).wait_recv()
        return 0

    lax.fori_loop(1, 8, await_taps, 0)
    for copy in table_loads:
        copy.wait()

    def transform(block):
        return dot(forward[0], block) + dot(forward[1], block)

    def taps_transform(index, _):
        taps_spec[index] = transform(all_taps[pl.ds(2 * index, 2)].reshape(BLOCK, lanes))
        return 0

    lax.fori_loop(0, blocks, taps_transform, 0)
    lax.fori_loop(ranks - 1, ranks - 1 + window, await_body, 0)

    def await_head(step, _):
        head_copy(step, source_of(step)).wait_recv()
        return 0

    lax.fori_loop(1, ranks, await_head, 0)

    sublane = lax.broadcasted_iota(jnp.int32, (8, HALF), 0)
    scale = 1.0 / math.sqrt(ranks * ranks * rows)

    def part_transform(chunk, index):
        spec[index] = transform(incoming[chunk, pl.ds(2 * index, 2)].reshape(BLOCK, lanes))

    def rows_of(tile):
        real = pl.ds(pl.multiple_of(tile * 8, 8), 8)
        imag = pl.ds(pl.multiple_of(BLOCK + tile * 8, 8), 8)
        sign = jnp.where(tile < BLOCK // 16, 1.0, -1.0)
        return real, imag, sign, (sublane + tile * 8) == 0

    def put(b, real, imag, sign, now, last):
        at = slice((b % 2) * HALF, (b % 2 + 1) * HALF)
        if last is not None:
            joint[b // 2, real, at] = now[0] + sign * last[0]
            joint[b // 2, imag, at] = now[1] + sign * last[1]
        else:
            joint[b // 2, real, at], joint[b // 2, imag, at] = now

    def sum_products(pairs):
        total = None
        for a, b in pairs:
            total = a * b if total is None else total + a * b
        return total

    def mix_conv(chunk):
        own = slice(chunk * HALF, (chunk + 1) * HALF)

        def tile_step(tile, _):
            real, imag, sign, ends = rows_of(tile)
            p_r = [spec[b, real, 0:HALF] for b in range(blocks)]
            p_i = [spec[b, imag, 0:HALF] for b in range(blocks)]
            h_r = [taps_spec[b, real, own] for b in range(blocks)]
            h_i = [taps_spec[b, imag, own] for b in range(blocks)]
            p_s = [p_r[b] + p_i[b] for b in range(blocks)]
            h_s = [h_r[b] + h_i[b] for b in range(blocks)]
            last = None
            for b in range(blocks):
                rr = sum_products((p_r[i], h_r[b - i]) for i in range(b + 1))
                ii = sum_products((p_i[i], h_i[b - i]) for i in range(b + 1))
                ss = sum_products((p_s[i], h_s[b - i]) for i in range(b + 1))
                now = (rr - jnp.where(ends, 0.0, ii), jnp.where(ends, ii, ss - rr - ii))
                put(b, real, imag, sign, now, last)
                last = now
            return 0

        lax.fori_loop(0, BLOCK // 8, tile_step, 0)

    def mix_grad():
        def tile_step(tile, _):
            real, imag, sign, ends = rows_of(tile)
            p_r = [spec[b, real, 0:HALF] for b in range(blocks)]
            p_i = [spec[b, imag, 0:HALF] for b in range(blocks)]
            g_r = [spec[b, real, HALF:lanes] for b in range(blocks)]
            g_i = [spec[b, imag, HALF:lanes] for b in range(blocks)]
            p_d = [p_r[b] - p_i[b] for b in range(blocks)]
            g_s = [g_r[b] + g_i[b] for b in range(blocks)]
            last = None
            for b in reversed(range(blocks)):
                rr = sum_products((p_r[i], g_r[b + i]) for i in range(blocks - b))
                ii = sum_products((p_i[i], g_i[b + i]) for i in range(blocks - b))
                ss = sum_products((p_d[i], g_s[b + i]) for i in range(blocks - b))
                now = (rr + jnp.where(ends, 0.0, ii), jnp.where(ends, ii, ss - rr + ii))
                put(b, real, imag, sign, now, last)
                last = now
            return 0

        lax.fori_loop(0, BLOCK // 8, tile_step, 0)

    def back(pair):
        value = joint[pair]
        high = value.astype(BF16)
        low = (value - high.astype(F32)).astype(BF16)
        return dot(inverse[0], high) + dot(inverse[0], low) + dot(inverse[1], high)

    def back_conv(chunk, send):
        own = slice(chunk * HALF, (chunk + 1) * HALF)

        def pair_step(index, _):
            pair = (z + side - 1 - index) % side
            result = back(pair)
            for part in range(4):
                target = 4 * pair + part
                value = result[(part % 2) * HALF : (part % 2 + 1) * HALF, (part // 2) * HALF : (part // 2 + 1) * HALF]
                product = incoming[chunk, target, :, 0:HALF].astype(F32)
                conv_own[chunk, target] = (value + skip[:, own] * product).astype(BF16)
                if send:

                    @pl.when(target != ctx)
                    def _():
                        conv_copy(chunk, target, ctx).start()

            return 0

        lax.fori_loop(0, side, pair_step, 0)

    def back_grad(chunk):
        def pair_step(pair, _):
            result = back(pair)
            for part in range(4):
                value = result[(part % 2) * HALF : (part % 2 + 1) * HALF, (part // 2) * HALF : (part // 2 + 1) * HALF]
                grad[chunk, 4 * pair + part] = value * scale
            return 0

        lax.fori_loop(0, side, pair_step, 0)

    def reduce_copy(chunk, slot, source, target, device):
        return pltpu.make_async_remote_copy(
            src_ref=source, dst_ref=target, send_sem=red_send.at[chunk, slot],
            recv_sem=red_recv.at[chunk, slot], device_id={"dp": device},
        )

    def core_copy(chunk):
        return reduce_copy(chunk, 0, core_out.at[chunk], core_in.at[chunk], core_mate)

    def x_copy(chunk, i):
        device = ((x + i) % 4) * 4 + zh * 2 + core
        return reduce_copy(chunk, i, x_out.at[chunk, i - 1], x_in.at[chunk, i - 1], device)

    def z_copy(chunk):
        return reduce_copy(chunk, 4, z_out.at[chunk], z_in.at[chunk], z_mate)

    def core_stage(chunk):
        def part_step(index, _):
            core_out[chunk, index] = grad[chunk, 2 * index + 1 - core].astype(BF16)
            return 0

        lax.fori_loop(0, 8, part_step, 0)
        core_copy(chunk).start()

    def x_stage(chunk):
        core_copy(chunk).wait_recv()
        for i in (1, 2, 3):
            for half in (0, 1):
                j = 2 * ((x + i) % 4) + half
                x_out[chunk, i - 1, half] = (
                    grad[chunk, 2 * j + core] + core_in[chunk, j].astype(F32)
                ).astype(BF16)
            x_copy(chunk, i).start()

    def x_total(chunk, half):
        j = 2 * x + half
        total = grad[chunk, 2 * j + core] + core_in[chunk, j].astype(F32)
        for i in range(3):
            total = total + x_in[chunk, i, half].astype(F32)
        return total

    def z_stage(chunk):
        for i in (1, 2, 3):
            x_copy(chunk, i).wait_recv()
        z_out[chunk] = x_total(chunk, 1 - zh).astype(BF16)
        z_copy(chunk).start()

    def z_finish(chunk):
        z_copy(chunk).wait_recv()
        taps_grad[:, chunk * HALF : (chunk + 1) * HALF] = x_total(chunk, zh) + z_in[chunk].astype(F32)

    def first_transform(index, _):
        part_transform(0, index)
        return 0

    lax.fori_loop(0, blocks, first_transform, 0)
    mix_conv(0)
    back_conv(0, False)
    mix_grad()
    back_grad(0)
    core_stage(0)

    for far in (3, 2, 1, 0):

        def await_late(index, _):
            step = ranks - 1 - index
            late_copy(step, source_of(step)).wait_recv()
            conv_copy(0, target_of(step), ctx).start()
            return 0

        lax.fori_loop((3 - far) * side, min((4 - far) * side, ranks - 1), await_late, 0)
        from_z = (z + side - far) % side
        part_transform(1, 2 * from_z)
        part_transform(1, 2 * from_z + 1)
        if far == 3:
            x_stage(0)
        if far == 1:
            z_stage(0)

    mix_conv(1)
    back_conv(1, True)
    mix_grad()
    back_grad(1)
    core_stage(1)

    def gate_part(chunk, source, value):
        cols = pl.ds(pl.multiple_of((source * 2 + chunk) * HALF, HALF), HALF)
        mixed[:, cols] = (gate[:, cols] * value.astype(F32)).astype(BF16)

    def gate_step(chunk):
        def one(index, _):
            step = ranks - 1 - index
            source = source_of(step)
            conv_copy(chunk, target_of(1), source).wait_recv()
            gate_part(chunk, source, conv_in[source, chunk])
            return 0

        return one

    gate_part(0, ctx, conv_own[0, ctx])
    gate_part(1, ctx, conv_own[1, ctx])
    z_finish(0)
    x_stage(1)
    halo_copy.wait_send()

    def drain_taps(step, _):
        taps_copy(dp, step, z_mate).wait_send()
        return 0

    lax.fori_loop(0, 15, drain_taps, 0)

    def drain_parts(step, _):
        body_copy(step, ctx).wait_send()
        head_copy(step, ctx).wait_send()
        late_copy(step, ctx).wait_send()
        return 0

    lax.fori_loop(1, ranks, drain_parts, 0)
    z_stage(1)
    lax.fori_loop(0, ranks - 1, gate_step(0), 0)

    def drain_conv(chunk):
        def one(step, _):
            conv_copy(chunk, target_of(step), ctx).wait_send()
            return 0

        lax.fori_loop(1, ranks, one, 0)

    drain_conv(0)
    for chunk in range(2):
        core_copy(chunk).wait_send()
        for i in (1, 2, 3):
            x_copy(chunk, i).wait_send()
    z_copy(0).wait_send()
    lax.fori_loop(0, ranks - 1, gate_step(1), 0)
    drain_conv(1)
    z_finish(1)
    z_copy(1).wait_send()


def hand_over(mixed_in, grad_in, mixed, taps_grad, sems):
    stores = [
        pltpu.make_async_copy(mixed_in, mixed, sems.at[0]),
        pltpu.make_async_copy(grad_in, taps_grad, sems.at[1]),
    ]
    for store in stores:
        store.start()
    for store in stores:
        store.wait()


def per_device(projected, short_weight, filter_taps, skip_gain, upstream):
    rows, joined = projected.shape[1:]
    width = joined // 3
    ranks = 16
    lanes = 2 * HALF
    blocks = ranks * rows // BLOCK
    forward, inverse = (jnp.asarray(t) for t in make_tables())
    vmem = pl.BlockSpec(memory_space=pltpu.VMEM)
    anywhere = pl.BlockSpec(memory_space=pl.ANY)
    shapes = [
        jax.ShapeDtypeStruct((rows, width), BF16),
        jax.ShapeDtypeStruct((rows, lanes), F32),
    ]
    results = pl.pallas_call(
        functools.partial(kernel, WINDOW),
        out_shape=[pltpu.VMEM(shape.shape, shape.dtype) for shape in shapes],
        in_specs=[anywhere] * 7,
        out_specs=[vmem] * 2,
        scratch_shapes=[
            pltpu.VMEM((rows, joined), BF16),
            pltpu.VMEM((rows, width), BF16),
            pltpu.VMEM(short_weight.shape, F32),
            pltpu.VMEM((rows, lanes), F32),
            pltpu.VMEM((1, lanes), F32),
            pltpu.VMEM(forward.shape, BF16),
            pltpu.VMEM(inverse.shape, BF16),
            pltpu.VMEM((16, joined), BF16),
            pltpu.VMEM((16, joined // 8), F32),
            pltpu.VMEM((16, joined // 8), BF16),
            pltpu.VMEM((16, joined // 8), BF16),
            pltpu.VMEM((8, joined), F32),
            pltpu.VMEM((rows, width), F32),
            pltpu.VMEM((2, ranks, rows, lanes), BF16),
            pltpu.VMEM((2, ranks, rows, lanes), BF16),
            pltpu.VMEM((ranks, rows, lanes), BF16),
            pltpu.VMEM((blocks, 2 * BLOCK, lanes), F32),
            pltpu.VMEM((blocks, 2 * BLOCK, lanes), F32),
            pltpu.VMEM((blocks // 2, 2 * BLOCK, lanes), F32),
            pltpu.VMEM((2, ranks, rows, HALF), BF16),
            pltpu.VMEM((ranks, 2, rows, HALF), BF16),
            pltpu.VMEM((2, ranks, rows, HALF), F32),
            pltpu.VMEM((2, 8, rows, HALF), BF16),
            pltpu.VMEM((2, 8, rows, HALF), BF16),
            pltpu.VMEM((2, 3, 2, rows, HALF), BF16),
            pltpu.VMEM((2, 3, 2, rows, HALF), BF16),
            pltpu.VMEM((2, rows, HALF), BF16),
            pltpu.VMEM((2, rows, HALF), BF16),
            pltpu.SemaphoreType.DMA((4, 4)),
            pltpu.SemaphoreType.DMA((6,)),
            pltpu.SemaphoreType.DMA((2,)),
            pltpu.SemaphoreType.DMA((16,)),
            pltpu.SemaphoreType.DMA((16,)),
            pltpu.SemaphoreType.DMA((16,)),
            pltpu.SemaphoreType.DMA((16,)),
            pltpu.SemaphoreType.DMA((2, 16)),
            pltpu.SemaphoreType.DMA((2, 16)),
            pltpu.SemaphoreType.DMA((2, 16)),
            pltpu.SemaphoreType.DMA((16, 2)),
            pltpu.SemaphoreType.DMA((2, 5)),
            pltpu.SemaphoreType.DMA((2, 5)),
        ],
        compiler_params=pltpu.CompilerParams(
            collective_id=0, has_side_effects=True, vmem_limit_bytes=60 * 2**20
        ),
    )(
        projected.reshape(rows, joined), short_weight, filter_taps, skip_gain.reshape(1, lanes),
        upstream.reshape(rows, width), forward, inverse,
    )
    mixed, taps_grad = pl.pallas_call(
        hand_over,
        out_shape=shapes,
        in_specs=[vmem] * 2,
        out_specs=[anywhere] * 2,
        scratch_shapes=[pltpu.SemaphoreType.DMA((2,))],
        compiler_params=pltpu.CompilerParams(vmem_limit_bytes=4 * 2**20),
    )(*results)
    return (mixed.reshape(1, rows, width), taps_grad)


def solution(mesh):
    in_specs = (P("dp", "ctx", None), P(), P("dp", "ctx"), P("ctx"), P("dp", "ctx", None))
    out_specs = (P("dp", "ctx", None), P("dp", "ctx"))
    return jax.shard_map(
        per_device, mesh=mesh, in_specs=in_specs, out_specs=out_specs, check_vma=False
    )
```

```python
import functools
import math

import jax
import jax.numpy as jnp
import ml_dtypes
import numpy as np
from jax import lax
from jax.experimental import pallas as pl
from jax.experimental.pallas import tpu as pltpu
from jax.sharding import PartitionSpec as P

SHORT = 3
BLOCK = 256
HALF = 128
WINDOW = 5
F32 = jnp.float32
BF16 = jnp.bfloat16


def split_table(table):
    high = table.astype(ml_dtypes.bfloat16)
    low = (table - high.astype(np.float64)).astype(ml_dtypes.bfloat16)
    return high, low


def make_tables():
    size = 2 * BLOCK
    freq = np.concatenate([np.arange(0, BLOCK, 2), np.arange(1, BLOCK, 2)])
    time = np.arange(BLOCK)
    angle = 2.0 * np.pi * ((freq[:, None] * time[None, :]) % size) / size
    real, imag = np.cos(angle), -np.sin(angle)
    imag[0] = np.where(time % 2 == 0, 1.0, -1.0)
    forward = np.concatenate([real, imag], axis=0)
    weight = np.full((size, 1), 2.0 / size)
    weight[0] = weight[BLOCK] = 1.0 / size
    inverse = (forward * weight).T
    return np.stack(split_table(forward)), np.stack(split_table(inverse))


def dot(a, b):
    return jnp.dot(a, b, preferred_element_type=F32)


def kernel(
    window, proj_hbm, weights_hbm, taps_hbm, skip_hbm, upstream_hbm, forward_hbm, inverse_hbm,
    mixed, taps_grad,
    proj, upstream, weights, taps, skip, forward, inverse, tail, pack, halo_out, halo_in, halo, gate,
    outgoing, incoming, all_taps, taps_spec, spec, joint, conv_own, conv_in, grad,
    core_out, core_in, x_out, x_in, z_out, z_in,
    load_sems, table_sems, halo_sems, taps_send, taps_recv, head_send, head_recv,
    part_send, part_recv, conv_send, conv_recv, red_send, red_recv,
):
    ctx, dp = lax.axis_index("ctx"), lax.axis_index("dp")
    ranks, side = 16, 4
    rows = proj.shape[0]
    width = proj.shape[1] // 3
    lanes = 2 * HALF
    blocks = ranks * rows // BLOCK
    z, y = ctx // side, ctx % side
    x, zh, core = dp // 4, (dp // 2) % 2, dp % 2
    z_mate = dp + 2 - 4 * zh
    core_mate = dp + 1 - 2 * core

    def target_of(step):
        return ((z + step // side) % side) * side + (y + step % side) % side

    def source_of(step):
        return ((z + side - step // side) % side) * side + (y + side - step % side) % side

    def plane_mate(step):
        return ((x + step // 2) % 4) * 4 + zh * 2 + (core + step % 2) % 2

    barrier = pltpu.get_barrier_semaphore()

    def greet(step, _):
        pl.semaphore_signal(barrier, inc=1, device_id={"ctx": target_of(step)})
        return 0

    def greet_plane(step, _):
        pl.semaphore_signal(barrier, inc=1, device_id={"dp": plane_mate(step)})
        return 0

    lax.fori_loop(1, ranks, greet, 0)
    lax.fori_loop(1, 8, greet_plane, 0)
    pl.semaphore_signal(barrier, inc=1, device_id={"dp": z_mate})

    group = side * lanes

    def loads_of(far):
        first = ((z + far) % side) * group
        copies = []
        for stream in range(3):
            cols = pl.ds(pl.multiple_of(stream * width + first, group), group)
            copies.append(
                pltpu.make_async_copy(proj_hbm.at[:, cols], proj.at[:, cols], load_sems.at[far, stream])
            )
        cols = pl.ds(pl.multiple_of(first, group), group)
        copies.append(
            pltpu.make_async_copy(upstream_hbm.at[:, cols], upstream.at[:, cols], load_sems.at[far, 3])
        )
        return copies

    weights_load = pltpu.make_async_copy(weights_hbm, weights, table_sems.at[3])
    weights_load.start()
    for copy in loads_of(3):
        copy.start()
    tail_load = pltpu.make_async_copy(proj_hbm.at[pl.ds(rows - 16, 16)], tail, table_sems.at[0])
    tail_load.start()
    taps_load = pltpu.make_async_copy(taps_hbm, taps, table_sems.at[4])
    taps_load.start()
    for far in (2, 1, 0):
        for copy in loads_of(far):
            copy.start()
    table_loads = [
        pltpu.make_async_copy(forward_hbm, forward, table_sems.at[1]),
        pltpu.make_async_copy(inverse_hbm, inverse, table_sems.at[2]),
        pltpu.make_async_copy(skip_hbm, skip, table_sems.at[5]),
    ]
    for copy in table_loads:
        copy.start()

    weights_load.wait()
    pl.semaphore_wait(barrier, ranks - 1 + 8)

    halo_copy = pltpu.make_async_remote_copy(
        src_ref=halo_out, dst_ref=halo_in, send_sem=halo_sems.at[0], recv_sem=halo_sems.at[1],
        device_id={"ctx": (ctx + 1) % ranks},
    )

    def taps_copy(block, slot, target):
        return pltpu.make_async_remote_copy(
            src_ref=all_taps.at[block], dst_ref=all_taps.at[block],
            send_sem=taps_send.at[slot], recv_sem=taps_recv.at[block], device_id={"dp": target},
        )

    def body_copy(step, landing):
        body = pl.ds(16, rows - 16)
        return pltpu.make_async_remote_copy(
            src_ref=outgoing.at[0, step, body], dst_ref=incoming.at[0, landing, body],
            send_sem=part_send.at[0, step], recv_sem=part_recv.at[0, landing],
            device_id={"ctx": target_of(step)},
        )

    def head_copy(step, landing):
        head = pl.ds(0, 16)
        return pltpu.make_async_remote_copy(
            src_ref=outgoing.at[0, step, head], dst_ref=incoming.at[0, landing, head],
            send_sem=head_send.at[step], recv_sem=head_recv.at[landing],
            device_id={"ctx": target_of(step)},
        )

    def late_copy(step, landing):
        return pltpu.make_async_remote_copy(
            src_ref=outgoing.at[1, step], dst_ref=incoming.at[1, landing],
            send_sem=part_send.at[1, step], recv_sem=part_recv.at[1, landing],
            device_id={"ctx": target_of(step)},
        )

    def conv_copy(chunk, target, landing):
        return pltpu.make_async_remote_copy(
            src_ref=conv_own.at[chunk, target], dst_ref=conv_in.at[landing, chunk],
            send_sem=conv_send.at[chunk, target], recv_sem=conv_recv.at[landing, chunk],
            device_id={"ctx": target},
        )

    def columns(first):
        return pl.ds(pl.multiple_of(first, lanes), lanes)

    def filtered(stream, first):
        cols = columns(stream * width + first)
        here = proj[:, cols].astype(F32)
        w = weights[:, cols]
        return w[0:1] * here + w[1:2] * pltpu.roll(here, 1, 0) + w[2:3] * pltpu.roll(here, 2, 0)

    head_row = lax.broadcasted_iota(jnp.int32, (16, lanes), 0)

    def filtered_head(stream, first):
        cols = columns(stream * width + first)
        here = proj[0:16, cols].astype(F32)
        older, old = halo[0:1, cols], halo[1:2, cols]
        back_one = jnp.where(head_row == 0, old, pltpu.roll(here, 1, 0))
        back_two = jnp.where(head_row == 0, older, jnp.where(head_row == 1, old, pltpu.roll(here, 2, 0)))
        w = weights[:, cols]
        return w[0:1] * here + w[1:2] * back_one + w[2:3] * back_two

    def make_parts(step, count, filter_rows):
        first = target_of(step) * lanes
        gate_q = filter_rows(0, first)
        product = (filter_rows(1, first) * filter_rows(2, first)).astype(BF16)
        cols = columns(first)
        gate[0:count, cols] = gate_q
        cotangent = (upstream[0:count, cols].astype(F32) * gate_q).astype(BF16)
        return [
            jnp.concatenate([product[:, lane : lane + HALF], cotangent[:, lane : lane + HALF]], axis=1)
            for lane in (0, HALF)
        ]

    def send_body(index, _):
        step = ranks - 1 - index
        parts = make_parts(step, rows, filtered)
        outgoing[0, step] = parts[0]
        outgoing[1, step] = parts[1]
        body_copy(step, ctx).start()
        return 0

    piece = 3 * width // 8
    for far in (3, 2, 1, 0):
        for copy in loads_of(far):
            copy.wait()
        lax.fori_loop((3 - far) * side, min((4 - far) * side, ranks - 1), send_body, 0)
        if far == 3:
            tail_load.wait()
            for seg in range(8):
                last = tail[:, seg * piece : (seg + 1) * piece].astype(F32)
                pack[2 * seg : 2 * seg + 2, :] = last[14:16]
            halo_out[...] = pack[...].astype(BF16)
            halo_copy.start()
            taps_load.wait()
            all_taps[dp] = taps[...].astype(BF16)
            taps_copy(dp, 0, z_mate).start()
    parts = make_parts(0, rows, filtered)
    incoming[0, ctx] = parts[0]
    incoming[1, ctx] = parts[1]

    def send_own(step, _):
        taps_copy(dp, step, plane_mate(step)).start()
        return 0

    lax.fori_loop(1, 8, send_own, 0)

    halo_copy.wait_recv()
    pack[...] = jnp.where(ctx > 0, halo_in[...].astype(F32), 0.0)
    for seg in range(8):
        halo[0:2, seg * piece : (seg + 1) * piece] = pack[2 * seg : 2 * seg + 2, :]

    def send_head(index, _):
        step = ranks - 1 - index
        parts = make_parts(step, 16, filtered_head)
        outgoing[0, step, 0:16] = parts[0]
        outgoing[1, step, 0:16] = parts[1]
        head_copy(step, ctx).start()
        return 0

    lax.fori_loop(0, ranks - 1, send_head, 0)
    parts = make_parts(0, 16, filtered_head)
    incoming[0, ctx, 0:16] = parts[0]
    incoming[1, ctx, 0:16] = parts[1]

    def spread(index):
        turn = index // 5
        return jnp.where(index % 5 == 4, 3 - turn, ranks - 1 - index + turn)

    def send_late(index, _):
        late_copy(spread(index), ctx).start()
        return 0

    def await_body(index, _):
        step = ranks - 1 - (index - window)
        body_copy(step, source_of(step)).wait_recv()
        return 0

    def await_and_send(index, _):
        await_body(index, 0)
        return send_late(index, 0)

    lax.fori_loop(0, window, send_late, 0)

    taps_copy(z_mate, 0, z_mate).wait_recv()

    def forward_taps(step, _):
        taps_copy(z_mate, 7 + step, plane_mate(step)).start()
        return 0

    lax.fori_loop(1, 8, forward_taps, 0)

    lax.fori_loop(window, ranks - 1, await_and_send, 0)

    def await_taps(step, _):
        taps_copy(plane_mate(step), 0, z_mate).wait_recv()
        taps_copy(plane_mate(step) + 2 - 4 * zh, 0, z_mate).wait_recv()
        return 0

    lax.fori_loop(1, 8, await_taps, 0)
    for copy in table_loads:
        copy.wait()

    def transform(block):
        return dot(forward[0], block) + dot(forward[1], block)

    def taps_transform(index, _):
        taps_spec[index] = transform(all_taps[pl.ds(2 * index, 2)].reshape(BLOCK, lanes))
        return 0

    lax.fori_loop(0, blocks, taps_transform, 0)
    lax.fori_loop(ranks - 1, ranks - 1 + window, await_body, 0)

    def await_head(step, _):
        head_copy(step, source_of(step)).wait_recv()
        return 0

    lax.fori_loop(1, ranks, await_head, 0)

    sublane = lax.broadcasted_iota(jnp.int32, (8, HALF), 0)
    scale = 1.0 / math.sqrt(ranks * ranks * rows)

    def part_transform(chunk, index):
        spec[index] = transform(incoming[chunk, pl.ds(2 * index, 2)].reshape(BLOCK, lanes))

    def rows_of(tile):
        real = pl.ds(pl.multiple_of(tile * 8, 8), 8)
        imag = pl.ds(pl.multiple_of(BLOCK + tile * 8, 8), 8)
        sign = jnp.where(tile < BLOCK // 16, 1.0, -1.0)
        return real, imag, sign, (sublane + tile * 8) == 0

    def put(b, real, imag, sign, now, last):
        at = slice((b % 2) * HALF, (b % 2 + 1) * HALF)
        if last is not None:
            joint[b // 2, real, at] = now[0] + sign * last[0]
            joint[b // 2, imag, at] = now[1] + sign * last[1]
        else:
            joint[b // 2, real, at], joint[b // 2, imag, at] = now

    def sum_products(pairs):
        total = None
        for a, b in pairs:
            total = a * b if total is None else total + a * b
        return total

    def mix_conv(chunk):
        own = slice(chunk * HALF, (chunk + 1) * HALF)

        def tile_step(tile, _):
            real, imag, sign, ends = rows_of(tile)
            p_r = [spec[b, real, 0:HALF] for b in range(blocks)]
            p_i = [spec[b, imag, 0:HALF] for b in range(blocks)]
            h_r = [taps_spec[b, real, own] for b in range(blocks)]
            h_i = [taps_spec[b, imag, own] for b in range(blocks)]
            p_s = [p_r[b] + p_i[b] for b in range(blocks)]
            h_s = [h_r[b] + h_i[b] for b in range(blocks)]
            last = None
            for b in range(blocks):
                rr = sum_products((p_r[i], h_r[b - i]) for i in range(b + 1))
                ii = sum_products((p_i[i], h_i[b - i]) for i in range(b + 1))
                ss = sum_products((p_s[i], h_s[b - i]) for i in range(b + 1))
                now = (rr - jnp.where(ends, 0.0, ii), jnp.where(ends, ii, ss - rr - ii))
                put(b, real, imag, sign, now, last)
                last = now
            return 0

        lax.fori_loop(0, BLOCK // 8, tile_step, 0)

    def mix_grad():
        def tile_step(tile, _):
            real, imag, sign, ends = rows_of(tile)
            p_r = [spec[b, real, 0:HALF] for b in range(blocks)]
            p_i = [spec[b, imag, 0:HALF] for b in range(blocks)]
            g_r = [spec[b, real, HALF:lanes] for b in range(blocks)]
            g_i = [spec[b, imag, HALF:lanes] for b in range(blocks)]
            p_d = [p_r[b] - p_i[b] for b in range(blocks)]
            g_s = [g_r[b] + g_i[b] for b in range(blocks)]
            last = None
            for b in reversed(range(blocks)):
                rr = sum_products((p_r[i], g_r[b + i]) for i in range(blocks - b))
                ii = sum_products((p_i[i], g_i[b + i]) for i in range(blocks - b))
                ss = sum_products((p_d[i], g_s[b + i]) for i in range(blocks - b))
                now = (rr + jnp.where(ends, 0.0, ii), jnp.where(ends, ii, ss - rr + ii))
                put(b, real, imag, sign, now, last)
                last = now
            return 0

        lax.fori_loop(0, BLOCK // 8, tile_step, 0)

    def back(pair):
        value = joint[pair]
        high = value.astype(BF16)
        low = (value - high.astype(F32)).astype(BF16)
        return dot(inverse[0], high) + dot(inverse[0], low) + dot(inverse[1], high)

    def back_conv(chunk, send):
        own = slice(chunk * HALF, (chunk + 1) * HALF)

        def pair_step(index, _):
            pair = (z + index) % side
            result = back(pair)
            for part in range(4):
                target = 4 * pair + part
                value = result[(part % 2) * HALF : (part % 2 + 1) * HALF, (part // 2) * HALF : (part // 2 + 1) * HALF]
                product = incoming[chunk, target, :, 0:HALF].astype(F32)
                conv_own[chunk, target] = (value + skip[:, own] * product).astype(BF16)
            if send:

                @pl.when(index > 0)
                def _():
                    for part in range(4):
                        conv_copy(chunk, 4 * pair + part, ctx).start()
                    conv_copy(chunk, target_of(index), ctx).start()

            return 0

        lax.fori_loop(0, side, pair_step, 0)

    def back_grad(chunk):
        def pair_step(pair, _):
            result = back(pair)
            for part in range(4):
                value = result[(part % 2) * HALF : (part % 2 + 1) * HALF, (part // 2) * HALF : (part // 2 + 1) * HALF]
                grad[chunk, 4 * pair + part] = value * scale
            return 0

        lax.fori_loop(0, side, pair_step, 0)

    def reduce_copy(chunk, slot, source, target, device):
        return pltpu.make_async_remote_copy(
            src_ref=source, dst_ref=target, send_sem=red_send.at[chunk, slot],
            recv_sem=red_recv.at[chunk, slot], device_id={"dp": device},
        )

    def core_copy(chunk):
        return reduce_copy(chunk, 0, core_out.at[chunk], core_in.at[chunk], core_mate)

    def x_copy(chunk, i):
        device = ((x + i) % 4) * 4 + zh * 2 + core
        return reduce_copy(chunk, i, x_out.at[chunk, i - 1], x_in.at[chunk, i - 1], device)

    def z_copy(chunk):
        return reduce_copy(chunk, 4, z_out.at[chunk], z_in.at[chunk], z_mate)

    def core_stage(chunk):
        def part_step(index, _):
            core_out[chunk, index] = grad[chunk, 2 * index + 1 - core].astype(BF16)
            return 0

        lax.fori_loop(0, 8, part_step, 0)
        core_copy(chunk).start()

    def x_stage(chunk):
        core_copy(chunk).wait_recv()
        for i in (1, 2, 3):
            for half in (0, 1):
                j = 2 * ((x + i) % 4) + half
                x_out[chunk, i - 1, half] = (
                    grad[chunk, 2 * j + core] + core_in[chunk, j].astype(F32)
                ).astype(BF16)
            x_copy(chunk, i).start()

    def x_total(chunk, half):
        j = 2 * x + half
        total = grad[chunk, 2 * j + core] + core_in[chunk, j].astype(F32)
        for i in range(3):
            total = total + x_in[chunk, i, half].astype(F32)
        return total

    def z_stage(chunk):
        for i in (1, 2, 3):
            x_copy(chunk, i).wait_recv()
        z_out[chunk] = x_total(chunk, 1 - zh).astype(BF16)
        z_copy(chunk).start()

    def z_finish(chunk):
        z_copy(chunk).wait_recv()
        taps_grad[:, chunk * HALF : (chunk + 1) * HALF] = x_total(chunk, zh) + z_in[chunk].astype(F32)

    def first_transform(index, _):
        part_transform(0, index)
        return 0

    lax.fori_loop(0, blocks, first_transform, 0)
    mix_conv(0)
    back_conv(0, False)
    mix_grad()
    back_grad(0)
    core_stage(0)

    for far in (3, 2, 1, 0):

        def await_late(index, _):
            step = ranks - 1 - index
            late_copy(step, source_of(step)).wait_recv()
            if far:
                conv_copy(0, target_of(step), ctx).start()
            return 0

        lax.fori_loop((3 - far) * side, min((4 - far) * side, ranks - 1), await_late, 0)
        if far:
            conv_copy(0, target_of(far), ctx).start()
        from_z = (z + side - far) % side
        part_transform(1, 2 * from_z)
        part_transform(1, 2 * from_z + 1)
        if far == 3:
            x_stage(0)

    mix_conv(1)
    back_conv(1, True)
    z_stage(0)
    mix_grad()
    back_grad(1)
    core_stage(1)
    x_stage(1)

    def gate_part(chunk, source, value):
        cols = pl.ds(pl.multiple_of((source * 2 + chunk) * HALF, HALF), HALF)
        mixed[:, cols] = (gate[:, cols] * value.astype(F32)).astype(BF16)

    def gate_step(chunk):
        def one(index, _):
            step = ranks - 1 - index
            source = source_of(step)
            conv_copy(chunk, target_of(1), source).wait_recv()
            gate_part(chunk, source, conv_in[source, chunk])
            return 0

        return one

    z_stage(1)
    gate_part(0, ctx, conv_own[0, ctx])
    gate_part(1, ctx, conv_own[1, ctx])
    z_finish(0)
    halo_copy.wait_send()

    def drain_taps(step, _):
        taps_copy(dp, step, z_mate).wait_send()
        return 0

    lax.fori_loop(0, 15, drain_taps, 0)

    def drain_parts(step, _):
        body_copy(step, ctx).wait_send()
        head_copy(step, ctx).wait_send()
        late_copy(step, ctx).wait_send()
        return 0

    lax.fori_loop(1, ranks, drain_parts, 0)
    lax.fori_loop(0, ranks - 1, gate_step(0), 0)

    def drain_conv(chunk):
        def one(step, _):
            conv_copy(chunk, target_of(step), ctx).wait_send()
            return 0

        lax.fori_loop(1, ranks, one, 0)

    drain_conv(0)
    for chunk in range(2):
        core_copy(chunk).wait_send()
        for i in (1, 2, 3):
            x_copy(chunk, i).wait_send()
    z_copy(0).wait_send()
    lax.fori_loop(0, ranks - 1, gate_step(1), 0)
    drain_conv(1)
    z_finish(1)
    z_copy(1).wait_send()


def hand_over(mixed_in, grad_in, mixed, taps_grad, sems):
    stores = [
        pltpu.make_async_copy(mixed_in, mixed, sems.at[0]),
        pltpu.make_async_copy(grad_in, taps_grad, sems.at[1]),
    ]
    for store in stores:
        store.start()
    for store in stores:
        store.wait()


def per_device(projected, short_weight, filter_taps, skip_gain, upstream):
    rows, joined = projected.shape[1:]
    width = joined // 3
    ranks = 16
    lanes = 2 * HALF
    blocks = ranks * rows // BLOCK
    forward, inverse = (jnp.asarray(t) for t in make_tables())
    vmem = pl.BlockSpec(memory_space=pltpu.VMEM)
    anywhere = pl.BlockSpec(memory_space=pl.ANY)
    shapes = [
        jax.ShapeDtypeStruct((rows, width), BF16),
        jax.ShapeDtypeStruct((rows, lanes), F32),
    ]
    results = pl.pallas_call(
        functools.partial(kernel, WINDOW),
        out_shape=[pltpu.VMEM(shape.shape, shape.dtype) for shape in shapes],
        in_specs=[anywhere] * 7,
        out_specs=[vmem] * 2,
        scratch_shapes=[
            pltpu.VMEM((rows, joined), BF16),
            pltpu.VMEM((rows, width), BF16),
            pltpu.VMEM(short_weight.shape, F32),
            pltpu.VMEM((rows, lanes), F32),
            pltpu.VMEM((1, lanes), F32),
            pltpu.VMEM(forward.shape, BF16),
            pltpu.VMEM(inverse.shape, BF16),
            pltpu.VMEM((16, joined), BF16),
            pltpu.VMEM((16, joined // 8), F32),
            pltpu.VMEM((16, joined // 8), BF16),
            pltpu.VMEM((16, joined // 8), BF16),
            pltpu.VMEM((8, joined), F32),
            pltpu.VMEM((rows, width), F32),
            pltpu.VMEM((2, ranks, rows, lanes), BF16),
            pltpu.VMEM((2, ranks, rows, lanes), BF16),
            pltpu.VMEM((ranks, rows, lanes), BF16),
            pltpu.VMEM((blocks, 2 * BLOCK, lanes), F32),
            pltpu.VMEM((blocks, 2 * BLOCK, lanes), F32),
            pltpu.VMEM((blocks // 2, 2 * BLOCK, lanes), F32),
            pltpu.VMEM((2, ranks, rows, HALF), BF16),
            pltpu.VMEM((ranks, 2, rows, HALF), BF16),
            pltpu.VMEM((2, ranks, rows, HALF), F32),
            pltpu.VMEM((2, 8, rows, HALF), BF16),
            pltpu.VMEM((2, 8, rows, HALF), BF16),
            pltpu.VMEM((2, 3, 2, rows, HALF), BF16),
            pltpu.VMEM((2, 3, 2, rows, HALF), BF16),
            pltpu.VMEM((2, rows, HALF), BF16),
            pltpu.VMEM((2, rows, HALF), BF16),
            pltpu.SemaphoreType.DMA((4, 4)),
            pltpu.SemaphoreType.DMA((6,)),
            pltpu.SemaphoreType.DMA((2,)),
            pltpu.SemaphoreType.DMA((16,)),
            pltpu.SemaphoreType.DMA((16,)),
            pltpu.SemaphoreType.DMA((16,)),
            pltpu.SemaphoreType.DMA((16,)),
            pltpu.SemaphoreType.DMA((2, 16)),
            pltpu.SemaphoreType.DMA((2, 16)),
            pltpu.SemaphoreType.DMA((2, 16)),
            pltpu.SemaphoreType.DMA((16, 2)),
            pltpu.SemaphoreType.DMA((2, 5)),
            pltpu.SemaphoreType.DMA((2, 5)),
        ],
        compiler_params=pltpu.CompilerParams(
            collective_id=0, has_side_effects=True, vmem_limit_bytes=60 * 2**20
        ),
    )(
        projected.reshape(rows, joined), short_weight, filter_taps, skip_gain.reshape(1, lanes),
        upstream.reshape(rows, width), forward, inverse,
    )
    mixed, taps_grad = pl.pallas_call(
        hand_over,
        out_shape=shapes,
        in_specs=[vmem] * 2,
        out_specs=[anywhere] * 2,
        scratch_shapes=[pltpu.SemaphoreType.DMA((2,))],
        compiler_params=pltpu.CompilerParams(vmem_limit_bytes=4 * 2**20),
    )(*results)
    return (mixed.reshape(1, rows, width), taps_grad)


def solution(mesh):
    in_specs = (P("dp", "ctx", None), P(), P("dp", "ctx"), P("ctx"), P("dp", "ctx", None))
    out_specs = (P("dp", "ctx", None), P("dp", "ctx"))
    return jax.shard_map(
        per_device, mesh=mesh, in_specs=in_specs, out_specs=out_specs, check_vma=False
    )
```

```python
import functools
import math

import jax
import jax.numpy as jnp
import ml_dtypes
import numpy as np
from jax import lax
from jax.experimental import pallas as pl
from jax.experimental.pallas import tpu as pltpu
from jax.sharding import PartitionSpec as P

SHORT = 3
BLOCK = 256
HALF = 128
WINDOW = 5
F32 = jnp.float32
BF16 = jnp.bfloat16


def split_table(table):
    high = table.astype(ml_dtypes.bfloat16)
    low = (table - high.astype(np.float64)).astype(ml_dtypes.bfloat16)
    return high, low


def make_tables():
    size = 2 * BLOCK
    freq = np.concatenate([np.arange(0, BLOCK, 2), np.arange(1, BLOCK, 2)])
    time = np.arange(BLOCK)
    angle = 2.0 * np.pi * ((freq[:, None] * time[None, :]) % size) / size
    real, imag = np.cos(angle), -np.sin(angle)
    imag[0] = np.where(time % 2 == 0, 1.0, -1.0)
    forward = np.concatenate([real, imag], axis=0)
    weight = np.full((size, 1), 2.0 / size)
    weight[0] = weight[BLOCK] = 1.0 / size
    inverse = (forward * weight).T
    return np.stack(split_table(forward)), np.stack(split_table(inverse))


def dot(a, b):
    return jnp.dot(a, b, preferred_element_type=F32)


def kernel(
    window, proj_hbm, weights_hbm, taps_hbm, skip_hbm, upstream_hbm, forward_hbm, inverse_hbm,
    mixed, taps_grad,
    proj, upstream, weights, taps, skip, forward, inverse, tail, pack, halo_out, halo_in, halo, gate,
    outgoing, incoming, all_taps, taps_spec, spec, joint, conv_own, conv_in, grad,
    core_out, core_in, x_out, x_in, z_out, z_in,
    load_sems, table_sems, halo_sems, taps_send, taps_recv, head_send, head_recv,
    part_send, part_recv, conv_send, conv_recv, red_send, red_recv,
):
    ctx, dp = lax.axis_index("ctx"), lax.axis_index("dp")
    ranks, side = 16, 4
    rows = proj.shape[0]
    width = proj.shape[1] // 3
    lanes = 2 * HALF
    blocks = ranks * rows // BLOCK
    z, y = ctx // side, ctx % side
    x, zh, core = dp // 4, (dp // 2) % 2, dp % 2
    z_mate = dp + 2 - 4 * zh
    core_mate = dp + 1 - 2 * core

    def target_of(step):
        return ((z + step // side) % side) * side + (y + step % side) % side

    def source_of(step):
        return ((z + side - step // side) % side) * side + (y + side - step % side) % side

    def plane_mate(step):
        return ((x + step // 2) % 4) * 4 + zh * 2 + (core + step % 2) % 2

    barrier = pltpu.get_barrier_semaphore()

    def greet(step, _):
        pl.semaphore_signal(barrier, inc=1, device_id={"ctx": target_of(step)})
        return 0

    def greet_plane(step, _):
        pl.semaphore_signal(barrier, inc=1, device_id={"dp": plane_mate(step)})
        return 0

    lax.fori_loop(1, ranks, greet, 0)
    lax.fori_loop(1, 8, greet_plane, 0)
    pl.semaphore_signal(barrier, inc=1, device_id={"dp": z_mate})

    group = side * lanes

    def loads_of(far):
        first = ((z + far) % side) * group
        copies = []
        for stream in range(3):
            cols = pl.ds(pl.multiple_of(stream * width + first, group), group)
            copies.append(
                pltpu.make_async_copy(proj_hbm.at[:, cols], proj.at[:, cols], load_sems.at[far, stream])
            )
        cols = pl.ds(pl.multiple_of(first, group), group)
        copies.append(
            pltpu.make_async_copy(upstream_hbm.at[:, cols], upstream.at[:, cols], load_sems.at[far, 3])
        )
        return copies

    weights_load = pltpu.make_async_copy(weights_hbm, weights, table_sems.at[3])
    weights_load.start()
    for copy in loads_of(3):
        copy.start()
    tail_load = pltpu.make_async_copy(proj_hbm.at[pl.ds(rows - 16, 16)], tail, table_sems.at[0])
    tail_load.start()
    taps_load = pltpu.make_async_copy(taps_hbm, taps, table_sems.at[4])
    taps_load.start()
    for far in (2, 1, 0):
        for copy in loads_of(far):
            copy.start()
    table_loads = [
        pltpu.make_async_copy(forward_hbm, forward, table_sems.at[1]),
        pltpu.make_async_copy(inverse_hbm, inverse, table_sems.at[2]),
        pltpu.make_async_copy(skip_hbm, skip, table_sems.at[5]),
    ]
    for copy in table_loads:
        copy.start()

    weights_load.wait()
    pl.semaphore_wait(barrier, ranks - 1 + 8)

    halo_copy = pltpu.make_async_remote_copy(
        src_ref=halo_out, dst_ref=halo_in, send_sem=halo_sems.at[0], recv_sem=halo_sems.at[1],
        device_id={"ctx": (ctx + 1) % ranks},
    )

    def taps_copy(block, slot, target):
        return pltpu.make_async_remote_copy(
            src_ref=all_taps.at[block], dst_ref=all_taps.at[block],
            send_sem=taps_send.at[slot], recv_sem=taps_recv.at[block], device_id={"dp": target},
        )

    def body_copy(step, landing):
        body = pl.ds(16, rows - 16)
        return pltpu.make_async_remote_copy(
            src_ref=outgoing.at[0, step, body], dst_ref=incoming.at[0, landing, body],
            send_sem=part_send.at[0, step], recv_sem=part_recv.at[0, landing],
            device_id={"ctx": target_of(step)},
        )

    def head_copy(step, landing):
        head = pl.ds(0, 16)
        return pltpu.make_async_remote_copy(
            src_ref=outgoing.at[0, step, head], dst_ref=incoming.at[0, landing, head],
            send_sem=head_send.at[step], recv_sem=head_recv.at[landing],
            device_id={"ctx": target_of(step)},
        )

    def late_copy(step, landing):
        return pltpu.make_async_remote_copy(
            src_ref=outgoing.at[1, step], dst_ref=incoming.at[1, landing],
            send_sem=part_send.at[1, step], recv_sem=part_recv.at[1, landing],
            device_id={"ctx": target_of(step)},
        )

    def conv_copy(chunk, target, landing):
        return pltpu.make_async_remote_copy(
            src_ref=conv_own.at[chunk, target], dst_ref=conv_in.at[landing, chunk],
            send_sem=conv_send.at[chunk, target], recv_sem=conv_recv.at[landing, chunk],
            device_id={"ctx": target},
        )

    def columns(first):
        return pl.ds(pl.multiple_of(first, lanes), lanes)

    def filtered(stream, first):
        cols = columns(stream * width + first)
        here = proj[:, cols].astype(F32)
        w = weights[:, cols]
        return w[0:1] * here + w[1:2] * pltpu.roll(here, 1, 0) + w[2:3] * pltpu.roll(here, 2, 0)

    head_row = lax.broadcasted_iota(jnp.int32, (16, lanes), 0)

    def filtered_head(stream, first):
        cols = columns(stream * width + first)
        here = proj[0:16, cols].astype(F32)
        older, old = halo[0:1, cols], halo[1:2, cols]
        back_one = jnp.where(head_row == 0, old, pltpu.roll(here, 1, 0))
        back_two = jnp.where(head_row == 0, older, jnp.where(head_row == 1, old, pltpu.roll(here, 2, 0)))
        w = weights[:, cols]
        return w[0:1] * here + w[1:2] * back_one + w[2:3] * back_two

    def make_parts(step, count, filter_rows):
        first = target_of(step) * lanes
        gate_q = filter_rows(0, first)
        product = (filter_rows(1, first) * filter_rows(2, first)).astype(BF16)
        cols = columns(first)
        gate[0:count, cols] = gate_q
        cotangent = (upstream[0:count, cols].astype(F32) * gate_q).astype(BF16)
        return [
            jnp.concatenate([product[:, lane : lane + HALF], cotangent[:, lane : lane + HALF]], axis=1)
            for lane in (0, HALF)
        ]

    def send_body(index, _):
        step = ranks - 1 - index
        parts = make_parts(step, rows, filtered)
        outgoing[0, step] = parts[0]
        outgoing[1, step] = parts[1]
        body_copy(step, ctx).start()
        return 0

    piece = 3 * width // 8
    for far in (3, 2, 1, 0):
        for copy in loads_of(far):
            copy.wait()
        lax.fori_loop((3 - far) * side, min((4 - far) * side, ranks - 1), send_body, 0)
        if far == 3:
            tail_load.wait()
            for seg in range(8):
                last = tail[:, seg * piece : (seg + 1) * piece].astype(F32)
                pack[2 * seg : 2 * seg + 2, :] = last[14:16]
            halo_out[...] = pack[...].astype(BF16)
            halo_copy.start()
            taps_load.wait()
            all_taps[dp] = taps[...].astype(BF16)
            taps_copy(dp, 0, z_mate).start()
    parts = make_parts(0, rows, filtered)
    incoming[0, ctx] = parts[0]
    incoming[1, ctx] = parts[1]

    def send_own(step, _):
        taps_copy(dp, step, plane_mate(step)).start()
        return 0


    halo_copy.wait_recv()
    pack[...] = jnp.where(ctx > 0, halo_in[...].astype(F32), 0.0)
    for seg in range(8):
        halo[0:2, seg * piece : (seg + 1) * piece] = pack[2 * seg : 2 * seg + 2, :]

    def send_head(index, _):
        step = ranks - 1 - index
        parts = make_parts(step, 16, filtered_head)
        outgoing[0, step, 0:16] = parts[0]
        outgoing[1, step, 0:16] = parts[1]
        head_copy(step, ctx).start()
        return 0

    lax.fori_loop(0, ranks - 1, send_head, 0)
    parts = make_parts(0, 16, filtered_head)
    incoming[0, ctx, 0:16] = parts[0]
    incoming[1, ctx, 0:16] = parts[1]

    def spread(index):
        turn = index // 5
        return jnp.where(index % 5 == 4, 3 - turn, ranks - 1 - index + turn)

    def send_late(index, _):
        late_copy(spread(index), ctx).start()
        return 0

    def await_body(index, _):
        step = ranks - 1 - (index - window)
        body_copy(step, source_of(step)).wait_recv()
        return 0

    def await_and_send(index, _):
        await_body(index, 0)
        return send_late(index, 0)

    lax.fori_loop(0, window, send_late, 0)

    taps_copy(z_mate, 0, z_mate).wait_recv()

    def forward_taps(step, _):
        taps_copy(z_mate, 7 + step, plane_mate(step)).start()
        return 0


    lax.fori_loop(window, 9, await_and_send, 0)
    lax.fori_loop(1, 8, send_own, 0)
    lax.fori_loop(1, 8, forward_taps, 0)
    lax.fori_loop(9, ranks - 1, await_and_send, 0)

    def await_taps(step, _):
        taps_copy(plane_mate(step), 0, z_mate).wait_recv()
        taps_copy(plane_mate(step) + 2 - 4 * zh, 0, z_mate).wait_recv()
        return 0

    lax.fori_loop(1, 8, await_taps, 0)
    for copy in table_loads:
        copy.wait()

    def transform(block):
        return dot(forward[0], block) + dot(forward[1], block)

    def taps_transform(index, _):
        taps_spec[index] = transform(all_taps[pl.ds(2 * index, 2)].reshape(BLOCK, lanes))
        return 0

    lax.fori_loop(0, blocks, taps_transform, 0)
    lax.fori_loop(ranks - 1, ranks - 1 + window, await_body, 0)

    def await_head(step, _):
        head_copy(step, source_of(step)).wait_recv()
        return 0

    lax.fori_loop(1, ranks, await_head, 0)

    sublane = lax.broadcasted_iota(jnp.int32, (8, HALF), 0)
    scale = 1.0 / math.sqrt(ranks * ranks * rows)

    def part_transform(chunk, index):
        spec[index] = transform(incoming[chunk, pl.ds(2 * index, 2)].reshape(BLOCK, lanes))

    def rows_of(tile):
        real = pl.ds(pl.multiple_of(tile * 8, 8), 8)
        imag = pl.ds(pl.multiple_of(BLOCK + tile * 8, 8), 8)
        sign = jnp.where(tile < BLOCK // 16, 1.0, -1.0)
        return real, imag, sign, (sublane + tile * 8) == 0

    def put(b, real, imag, sign, now, last):
        at = slice((b % 2) * HALF, (b % 2 + 1) * HALF)
        if last is not None:
            joint[b // 2, real, at] = now[0] + sign * last[0]
            joint[b // 2, imag, at] = now[1] + sign * last[1]
        else:
            joint[b // 2, real, at], joint[b // 2, imag, at] = now

    def sum_products(pairs):
        total = None
        for a, b in pairs:
            total = a * b if total is None else total + a * b
        return total

    def mix_conv(chunk):
        own = slice(chunk * HALF, (chunk + 1) * HALF)

        def tile_step(tile, _):
            real, imag, sign, ends = rows_of(tile)
            p_r = [spec[b, real, 0:HALF] for b in range(blocks)]
            p_i = [spec[b, imag, 0:HALF] for b in range(blocks)]
            h_r = [taps_spec[b, real, own] for b in range(blocks)]
            h_i = [taps_spec[b, imag, own] for b in range(blocks)]
            p_s = [p_r[b] + p_i[b] for b in range(blocks)]
            h_s = [h_r[b] + h_i[b] for b in range(blocks)]
            last = None
            for b in range(blocks):
                rr = sum_products((p_r[i], h_r[b - i]) for i in range(b + 1))
                ii = sum_products((p_i[i], h_i[b - i]) for i in range(b + 1))
                ss = sum_products((p_s[i], h_s[b - i]) for i in range(b + 1))
                now = (rr - jnp.where(ends, 0.0, ii), jnp.where(ends, ii, ss - rr - ii))
                put(b, real, imag, sign, now, last)
                last = now
            return 0

        lax.fori_loop(0, BLOCK // 8, tile_step, 0)

    def mix_grad():
        def tile_step(tile, _):
            real, imag, sign, ends = rows_of(tile)
            p_r = [spec[b, real, 0:HALF] for b in range(blocks)]
            p_i = [spec[b, imag, 0:HALF] for b in range(blocks)]
            g_r = [spec[b, real, HALF:lanes] for b in range(blocks)]
            g_i = [spec[b, imag, HALF:lanes] for b in range(blocks)]
            p_d = [p_r[b] - p_i[b] for b in range(blocks)]
            g_s = [g_r[b] + g_i[b] for b in range(blocks)]
            last = None
            for b in reversed(range(blocks)):
                rr = sum_products((p_r[i], g_r[b + i]) for i in range(blocks - b))
                ii = sum_products((p_i[i], g_i[b + i]) for i in range(blocks - b))
                ss = sum_products((p_d[i], g_s[b + i]) for i in range(blocks - b))
                now = (rr + jnp.where(ends, 0.0, ii), jnp.where(ends, ii, ss - rr + ii))
                put(b, real, imag, sign, now, last)
                last = now
            return 0

        lax.fori_loop(0, BLOCK // 8, tile_step, 0)

    def back(pair):
        value = joint[pair]
        high = value.astype(BF16)
        low = (value - high.astype(F32)).astype(BF16)
        return dot(inverse[0], high) + dot(inverse[0], low) + dot(inverse[1], high)

    def back_conv(chunk, send):
        own = slice(chunk * HALF, (chunk + 1) * HALF)

        def pair_step(index, _):
            pair = (z + index) % side
            result = back(pair)
            for part in range(4):
                target = 4 * pair + part
                value = result[(part % 2) * HALF : (part % 2 + 1) * HALF, (part // 2) * HALF : (part // 2 + 1) * HALF]
                product = incoming[chunk, target, :, 0:HALF].astype(F32)
                conv_own[chunk, target] = (value + skip[:, own] * product).astype(BF16)
            if send:

                @pl.when(index > 0)
                def _():
                    for part in range(4):
                        conv_copy(chunk, 4 * pair + part, ctx).start()
                    conv_copy(chunk, target_of(index), ctx).start()

            return 0

        lax.fori_loop(0, side, pair_step, 0)

    def back_grad(chunk):
        def pair_step(pair, _):
            result = back(pair)
            for part in range(4):
                value = result[(part % 2) * HALF : (part % 2 + 1) * HALF, (part // 2) * HALF : (part // 2 + 1) * HALF]
                grad[chunk, 4 * pair + part] = value * scale
            return 0

        lax.fori_loop(0, side, pair_step, 0)

    def reduce_copy(chunk, slot, source, target, device):
        return pltpu.make_async_remote_copy(
            src_ref=source, dst_ref=target, send_sem=red_send.at[chunk, slot],
            recv_sem=red_recv.at[chunk, slot], device_id={"dp": device},
        )

    def core_copy(chunk):
        return reduce_copy(chunk, 0, core_out.at[chunk], core_in.at[chunk], core_mate)

    def x_copy(chunk, i):
        device = ((x + i) % 4) * 4 + zh * 2 + core
        return reduce_copy(chunk, i, x_out.at[chunk, i - 1], x_in.at[chunk, i - 1], device)

    def z_copy(chunk):
        return reduce_copy(chunk, 4, z_out.at[chunk], z_in.at[chunk], z_mate)

    def core_stage(chunk):
        def part_step(index, _):
            core_out[chunk, index] = grad[chunk, 2 * index + 1 - core].astype(BF16)
            return 0

        lax.fori_loop(0, 8, part_step, 0)
        core_copy(chunk).start()

    def x_stage(chunk):
        core_copy(chunk).wait_recv()
        for i in (1, 2, 3):
            for half in (0, 1):
                j = 2 * ((x + i) % 4) + half
                x_out[chunk, i - 1, half] = (
                    grad[chunk, 2 * j + core] + core_in[chunk, j].astype(F32)
                ).astype(BF16)
            x_copy(chunk, i).start()

    def x_total(chunk, half):
        j = 2 * x + half
        total = grad[chunk, 2 * j + core] + core_in[chunk, j].astype(F32)
        for i in range(3):
            total = total + x_in[chunk, i, half].astype(F32)
        return total

    def z_stage(chunk):
        for i in (1, 2, 3):
            x_copy(chunk, i).wait_recv()
        z_out[chunk] = x_total(chunk, 1 - zh).astype(BF16)
        z_copy(chunk).start()

    def z_finish(chunk):
        z_copy(chunk).wait_recv()
        taps_grad[:, chunk * HALF : (chunk + 1) * HALF] = x_total(chunk, zh) + z_in[chunk].astype(F32)

    def first_transform(index, _):
        part_transform(0, index)
        return 0

    lax.fori_loop(0, blocks, first_transform, 0)
    mix_conv(0)
    back_conv(0, False)
    mix_grad()
    back_grad(0)
    core_stage(0)

    for far in (3, 2, 1, 0):

        def await_late(index, _):
            step = ranks - 1 - index
            late_copy(step, source_of(step)).wait_recv()
            if far:
                conv_copy(0, target_of(step), ctx).start()
            return 0

        lax.fori_loop((3 - far) * side, min((4 - far) * side, ranks - 1), await_late, 0)
        if far:
            conv_copy(0, target_of(far), ctx).start()
        from_z = (z + side - far) % side
        part_transform(1, 2 * from_z)
        part_transform(1, 2 * from_z + 1)
        if far == 3:
            x_stage(0)

    mix_conv(1)
    back_conv(1, True)
    z_stage(0)
    mix_grad()
    back_grad(1)
    core_stage(1)
    x_stage(1)

    def gate_part(chunk, source, value):
        cols = pl.ds(pl.multiple_of((source * 2 + chunk) * HALF, HALF), HALF)
        mixed[:, cols] = (gate[:, cols] * value.astype(F32)).astype(BF16)

    def gate_step(chunk):
        def one(index, _):
            step = ranks - 1 - index
            source = source_of(step)
            conv_copy(chunk, target_of(1), source).wait_recv()
            gate_part(chunk, source, conv_in[source, chunk])
            return 0

        return one

    z_stage(1)
    gate_part(0, ctx, conv_own[0, ctx])
    gate_part(1, ctx, conv_own[1, ctx])
    z_finish(0)
    halo_copy.wait_send()

    def drain_taps(step, _):
        taps_copy(dp, step, z_mate).wait_send()
        return 0

    lax.fori_loop(0, 15, drain_taps, 0)

    def drain_parts(step, _):
        body_copy(step, ctx).wait_send()
        head_copy(step, ctx).wait_send()
        late_copy(step, ctx).wait_send()
        return 0

    lax.fori_loop(1, ranks, drain_parts, 0)
    lax.fori_loop(0, ranks - 1, gate_step(0), 0)

    def drain_conv(chunk):
        def one(step, _):
            conv_copy(chunk, target_of(step), ctx).wait_send()
            return 0

        lax.fori_loop(1, ranks, one, 0)

    drain_conv(0)
    for chunk in range(2):
        core_copy(chunk).wait_send()
        for i in (1, 2, 3):
            x_copy(chunk, i).wait_send()
    z_copy(0).wait_send()
    lax.fori_loop(0, ranks - 1, gate_step(1), 0)
    drain_conv(1)
    z_finish(1)
    z_copy(1).wait_send()


def hand_over(mixed_in, grad_in, mixed, taps_grad, sems):
    parts = 4
    rows = mixed.shape[0] // parts
    stores = [pltpu.make_async_copy(grad_in, taps_grad, sems.at[parts])]
    for part in range(parts):
        own = pl.ds(part * rows, rows)
        stores.append(pltpu.make_async_copy(mixed_in.at[own], mixed.at[own], sems.at[part]))
    for store in stores:
        store.start()
    for store in stores:
        store.wait()


def per_device(projected, short_weight, filter_taps, skip_gain, upstream):
    rows, joined = projected.shape[1:]
    width = joined // 3
    ranks = 16
    lanes = 2 * HALF
    blocks = ranks * rows // BLOCK
    forward, inverse = (jnp.asarray(t) for t in make_tables())
    vmem = pl.BlockSpec(memory_space=pltpu.VMEM)
    anywhere = pl.BlockSpec(memory_space=pl.ANY)
    shapes = [
        jax.ShapeDtypeStruct((rows, width), BF16),
        jax.ShapeDtypeStruct((rows, lanes), F32),
    ]
    results = pl.pallas_call(
        functools.partial(kernel, WINDOW),
        out_shape=[pltpu.VMEM(shape.shape, shape.dtype) for shape in shapes],
        in_specs=[anywhere] * 7,
        out_specs=[vmem] * 2,
        scratch_shapes=[
            pltpu.VMEM((rows, joined), BF16),
            pltpu.VMEM((rows, width), BF16),
            pltpu.VMEM(short_weight.shape, F32),
            pltpu.VMEM((rows, lanes), F32),
            pltpu.VMEM((1, lanes), F32),
            pltpu.VMEM(forward.shape, BF16),
            pltpu.VMEM(inverse.shape, BF16),
            pltpu.VMEM((16, joined), BF16),
            pltpu.VMEM((16, joined // 8), F32),
            pltpu.VMEM((16, joined // 8), BF16),
            pltpu.VMEM((16, joined // 8), BF16),
            pltpu.VMEM((8, joined), F32),
            pltpu.VMEM((rows, width), F32),
            pltpu.VMEM((2, ranks, rows, lanes), BF16),
            pltpu.VMEM((2, ranks, rows, lanes), BF16),
            pltpu.VMEM((ranks, rows, lanes), BF16),
            pltpu.VMEM((blocks, 2 * BLOCK, lanes), F32),
            pltpu.VMEM((blocks, 2 * BLOCK, lanes), F32),
            pltpu.VMEM((blocks // 2, 2 * BLOCK, lanes), F32),
            pltpu.VMEM((2, ranks, rows, HALF), BF16),
            pltpu.VMEM((ranks, 2, rows, HALF), BF16),
            pltpu.VMEM((2, ranks, rows, HALF), F32),
            pltpu.VMEM((2, 8, rows, HALF), BF16),
            pltpu.VMEM((2, 8, rows, HALF), BF16),
            pltpu.VMEM((2, 3, 2, rows, HALF), BF16),
            pltpu.VMEM((2, 3, 2, rows, HALF), BF16),
            pltpu.VMEM((2, rows, HALF), BF16),
            pltpu.VMEM((2, rows, HALF), BF16),
            pltpu.SemaphoreType.DMA((4, 4)),
            pltpu.SemaphoreType.DMA((6,)),
            pltpu.SemaphoreType.DMA((2,)),
            pltpu.SemaphoreType.DMA((16,)),
            pltpu.SemaphoreType.DMA((16,)),
            pltpu.SemaphoreType.DMA((16,)),
            pltpu.SemaphoreType.DMA((16,)),
            pltpu.SemaphoreType.DMA((2, 16)),
            pltpu.SemaphoreType.DMA((2, 16)),
            pltpu.SemaphoreType.DMA((2, 16)),
            pltpu.SemaphoreType.DMA((16, 2)),
            pltpu.SemaphoreType.DMA((2, 5)),
            pltpu.SemaphoreType.DMA((2, 5)),
        ],
        compiler_params=pltpu.CompilerParams(
            collective_id=0, has_side_effects=True, vmem_limit_bytes=60 * 2**20
        ),
    )(
        projected.reshape(rows, joined), short_weight, filter_taps, skip_gain.reshape(1, lanes),
        upstream.reshape(rows, width), forward, inverse,
    )
    mixed, taps_grad = pl.pallas_call(
        hand_over,
        out_shape=shapes,
        in_specs=[vmem] * 2,
        out_specs=[anywhere] * 2,
        scratch_shapes=[pltpu.SemaphoreType.DMA((5,))],
        compiler_params=pltpu.CompilerParams(vmem_limit_bytes=4 * 2**20),
    )(*results)
    return (mixed.reshape(1, rows, width), taps_grad)


def solution(mesh):
    in_specs = (P("dp", "ctx", None), P(), P("dp", "ctx"), P("ctx"), P("dp", "ctx", None))
    out_specs = (P("dp", "ctx", None), P("dp", "ctx"))
    return jax.shard_map(
        per_device, mesh=mesh, in_specs=in_specs, out_specs=out_specs, check_vma=False
    )
```

```python
import functools
import math

import jax
import jax.numpy as jnp
import ml_dtypes
import numpy as np
from jax import lax
from jax.experimental import pallas as pl
from jax.experimental.pallas import tpu as pltpu
from jax.sharding import PartitionSpec as P

SHORT = 3
BLOCK = 256
HALF = 128
WINDOW = 5
F32 = jnp.float32
BF16 = jnp.bfloat16


def split_table(table):
    high = table.astype(ml_dtypes.bfloat16)
    low = (table - high.astype(np.float64)).astype(ml_dtypes.bfloat16)
    return high, low


def make_tables():
    size = 2 * BLOCK
    freq = np.concatenate([np.arange(0, BLOCK, 2), np.arange(1, BLOCK, 2)])
    time = np.arange(BLOCK)
    angle = 2.0 * np.pi * ((freq[:, None] * time[None, :]) % size) / size
    real, imag = np.cos(angle), -np.sin(angle)
    imag[0] = np.where(time % 2 == 0, 1.0, -1.0)
    forward = np.concatenate([real, imag], axis=0)
    weight = np.full((size, 1), 2.0 / size)
    weight[0] = weight[BLOCK] = 1.0 / size
    inverse = (forward * weight).T
    return np.stack(split_table(forward)), np.stack(split_table(inverse))


def dot(a, b):
    return jnp.dot(a, b, preferred_element_type=F32)


def kernel(
    window, proj_hbm, weights_hbm, taps_hbm, skip_hbm, upstream_hbm, forward_hbm, inverse_hbm,
    mixed, taps_grad,
    proj, upstream, weights, taps, skip, forward, inverse, tail, pack, halo_out, halo_in, halo, gate,
    outgoing, incoming, all_taps, taps_spec, spec, joint, conv_own, conv_in, grad,
    core_out, core_in, x_out, x_in, z_out, z_in,
    load_sems, table_sems, halo_sems, taps_send, taps_recv, head_send, head_recv,
    part_send, part_recv, conv_send, conv_recv, red_send, red_recv,
):
    ctx, dp = lax.axis_index("ctx"), lax.axis_index("dp")
    ranks, side = 16, 4
    rows = proj.shape[0]
    width = proj.shape[1] // 3
    lanes = 2 * HALF
    blocks = ranks * rows // BLOCK
    z, y = ctx // side, ctx % side
    x, zh, core = dp // 4, (dp // 2) % 2, dp % 2
    z_mate = dp + 2 - 4 * zh
    core_mate = dp + 1 - 2 * core

    def target_of(step):
        return ((z + step // side) % side) * side + (y + step % side) % side

    def source_of(step):
        return ((z + side - step // side) % side) * side + (y + side - step % side) % side

    def plane_mate(step):
        return ((x + step // 2) % 4) * 4 + zh * 2 + (core + step % 2) % 2

    barrier = pltpu.get_barrier_semaphore()

    def greet(step, _):
        pl.semaphore_signal(barrier, inc=1, device_id={"ctx": target_of(step)})
        return 0

    def greet_plane(step, _):
        pl.semaphore_signal(barrier, inc=1, device_id={"dp": plane_mate(step)})
        return 0


    group = side * lanes

    def loads_of(far):
        first = ((z + far) % side) * group
        copies = []
        for stream in range(3):
            cols = pl.ds(pl.multiple_of(stream * width + first, group), group)
            copies.append(
                pltpu.make_async_copy(proj_hbm.at[:, cols], proj.at[:, cols], load_sems.at[far, stream])
            )
        cols = pl.ds(pl.multiple_of(first, group), group)
        copies.append(
            pltpu.make_async_copy(upstream_hbm.at[:, cols], upstream.at[:, cols], load_sems.at[far, 3])
        )
        return copies

    weights_load = pltpu.make_async_copy(weights_hbm, weights, table_sems.at[3])
    weights_load.start()
    for copy in loads_of(3):
        copy.start()
    lax.fori_loop(1, ranks, greet, 0)
    lax.fori_loop(1, 8, greet_plane, 0)
    pl.semaphore_signal(barrier, inc=1, device_id={"dp": z_mate})
    tail_load = pltpu.make_async_copy(proj_hbm.at[pl.ds(rows - 16, 16)], tail, table_sems.at[0])
    tail_load.start()
    taps_load = pltpu.make_async_copy(taps_hbm, taps, table_sems.at[4])
    taps_load.start()
    for far in (2, 1, 0):
        for copy in loads_of(far):
            copy.start()
    table_loads = [
        pltpu.make_async_copy(forward_hbm, forward, table_sems.at[1]),
        pltpu.make_async_copy(inverse_hbm, inverse, table_sems.at[2]),
        pltpu.make_async_copy(skip_hbm, skip, table_sems.at[5]),
    ]
    for copy in table_loads:
        copy.start()

    weights_load.wait()
    pl.semaphore_wait(barrier, ranks - 1 + 8)

    halo_copy = pltpu.make_async_remote_copy(
        src_ref=halo_out, dst_ref=halo_in, send_sem=halo_sems.at[0], recv_sem=halo_sems.at[1],
        device_id={"ctx": (ctx + 1) % ranks},
    )

    def taps_copy(block, slot, target):
        return pltpu.make_async_remote_copy(
            src_ref=all_taps.at[block], dst_ref=all_taps.at[block],
            send_sem=taps_send.at[slot], recv_sem=taps_recv.at[block], device_id={"dp": target},
        )

    def body_copy(step, landing):
        body = pl.ds(16, rows - 16)
        return pltpu.make_async_remote_copy(
            src_ref=outgoing.at[0, step, body], dst_ref=incoming.at[0, landing, body],
            send_sem=part_send.at[0, step], recv_sem=part_recv.at[0, landing],
            device_id={"ctx": target_of(step)},
        )

    def head_copy(step, landing):
        head = pl.ds(0, 16)
        return pltpu.make_async_remote_copy(
            src_ref=outgoing.at[0, step, head], dst_ref=incoming.at[0, landing, head],
            send_sem=head_send.at[step], recv_sem=head_recv.at[landing],
            device_id={"ctx": target_of(step)},
        )

    def late_copy(step, landing):
        return pltpu.make_async_remote_copy(
            src_ref=outgoing.at[1, step], dst_ref=incoming.at[1, landing],
            send_sem=part_send.at[1, step], recv_sem=part_recv.at[1, landing],
            device_id={"ctx": target_of(step)},
        )

    def conv_copy(chunk, target, landing):
        return pltpu.make_async_remote_copy(
            src_ref=conv_own.at[chunk, target], dst_ref=conv_in.at[landing, chunk],
            send_sem=conv_send.at[chunk, target], recv_sem=conv_recv.at[landing, chunk],
            device_id={"ctx": target},
        )

    def columns(first):
        return pl.ds(pl.multiple_of(first, lanes), lanes)

    def filtered(stream, first):
        cols = columns(stream * width + first)
        here = proj[:, cols].astype(F32)
        w = weights[:, cols]
        return w[0:1] * here + w[1:2] * pltpu.roll(here, 1, 0) + w[2:3] * pltpu.roll(here, 2, 0)

    head_row = lax.broadcasted_iota(jnp.int32, (16, lanes), 0)

    def filtered_head(stream, first):
        cols = columns(stream * width + first)
        here = proj[0:16, cols].astype(F32)
        older, old = halo[0:1, cols], halo[1:2, cols]
        back_one = jnp.where(head_row == 0, old, pltpu.roll(here, 1, 0))
        back_two = jnp.where(head_row == 0, older, jnp.where(head_row == 1, old, pltpu.roll(here, 2, 0)))
        w = weights[:, cols]
        return w[0:1] * here + w[1:2] * back_one + w[2:3] * back_two

    def make_parts(step, count, filter_rows):
        first = target_of(step) * lanes
        gate_q = filter_rows(0, first)
        product = (filter_rows(1, first) * filter_rows(2, first)).astype(BF16)
        cols = columns(first)
        gate[0:count, cols] = gate_q
        cotangent = (upstream[0:count, cols].astype(F32) * gate_q).astype(BF16)
        return [
            jnp.concatenate([product[:, lane : lane + HALF], cotangent[:, lane : lane + HALF]], axis=1)
            for lane in (0, HALF)
        ]

    def send_body(index, _):
        step = ranks - 1 - index
        parts = make_parts(step, rows, filtered)
        outgoing[0, step] = parts[0]
        outgoing[1, step] = parts[1]
        body_copy(step, ctx).start()
        return 0

    piece = 3 * width // 8
    for far in (3, 2, 1, 0):
        for copy in loads_of(far):
            copy.wait()
        lax.fori_loop((3 - far) * side, min((4 - far) * side, ranks - 1), send_body, 0)
        if far == 3:
            tail_load.wait()
            for seg in range(8):
                last = tail[:, seg * piece : (seg + 1) * piece].astype(F32)
                pack[2 * seg : 2 * seg + 2, :] = last[14:16]
            halo_out[...] = pack[...].astype(BF16)
            halo_copy.start()
            taps_load.wait()
            all_taps[dp] = taps[...].astype(BF16)
            taps_copy(dp, 0, z_mate).start()
    parts = make_parts(0, rows, filtered)
    incoming[0, ctx] = parts[0]
    incoming[1, ctx] = parts[1]

    def send_own(step, _):
        taps_copy(dp, step, plane_mate(step)).start()
        return 0

    lax.fori_loop(1, 8, send_own, 0)

    halo_copy.wait_recv()
    pack[...] = jnp.where(ctx > 0, halo_in[...].astype(F32), 0.0)
    for seg in range(8):
        halo[0:2, seg * piece : (seg + 1) * piece] = pack[2 * seg : 2 * seg + 2, :]

    def send_head(index, _):
        step = ranks - 1 - index
        parts = make_parts(step, 16, filtered_head)
        outgoing[0, step, 0:16] = parts[0]
        outgoing[1, step, 0:16] = parts[1]
        head_copy(step, ctx).start()
        return 0

    lax.fori_loop(0, ranks - 1, send_head, 0)
    parts = make_parts(0, 16, filtered_head)
    incoming[0, ctx, 0:16] = parts[0]
    incoming[1, ctx, 0:16] = parts[1]

    def spread(index):
        turn = index // 5
        return jnp.where(index % 5 == 4, 3 - turn, ranks - 1 - index + turn)

    def send_late(index, _):
        late_copy(spread(index), ctx).start()
        return 0

    def await_body(index, _):
        step = ranks - 1 - (index - window)
        body_copy(step, source_of(step)).wait_recv()
        return 0

    def await_and_send(index, _):
        await_body(index, 0)
        return send_late(index, 0)

    lax.fori_loop(0, window, send_late, 0)

    taps_copy(z_mate, 0, z_mate).wait_recv()

    def forward_taps(step, _):
        taps_copy(z_mate, 7 + step, plane_mate(step)).start()
        return 0

    lax.fori_loop(1, 8, forward_taps, 0)

    lax.fori_loop(window, ranks - 1, await_and_send, 0)

    def await_taps(step, _):
        taps_copy(plane_mate(step), 0, z_mate).wait_recv()
        taps_copy(plane_mate(step) + 2 - 4 * zh, 0, z_mate).wait_recv()
        return 0

    lax.fori_loop(1, 8, await_taps, 0)
    for copy in table_loads:
        copy.wait()

    def transform(block):
        return dot(forward[0], block) + dot(forward[1], block)

    def taps_transform(index, _):
        taps_spec[index] = transform(all_taps[pl.ds(2 * index, 2)].reshape(BLOCK, lanes))
        return 0

    lax.fori_loop(0, blocks, taps_transform, 0)
    lax.fori_loop(ranks - 1, ranks - 1 + window, await_body, 0)

    def await_head(step, _):
        head_copy(step, source_of(step)).wait_recv()
        return 0

    lax.fori_loop(1, ranks, await_head, 0)

    sublane = lax.broadcasted_iota(jnp.int32, (8, HALF), 0)
    scale = 1.0 / math.sqrt(ranks * ranks * rows)

    def part_transform(chunk, index):
        spec[index] = transform(incoming[chunk, pl.ds(2 * index, 2)].reshape(BLOCK, lanes))

    def rows_of(tile):
        real = pl.ds(pl.multiple_of(tile * 8, 8), 8)
        imag = pl.ds(pl.multiple_of(BLOCK + tile * 8, 8), 8)
        sign = jnp.where(tile < BLOCK // 16, 1.0, -1.0)
        return real, imag, sign, (sublane + tile * 8) == 0

    def put(b, real, imag, sign, now, last):
        at = slice((b % 2) * HALF, (b % 2 + 1) * HALF)
        if last is not None:
            joint[b // 2, real, at] = now[0] + sign * last[0]
            joint[b // 2, imag, at] = now[1] + sign * last[1]
        else:
            joint[b // 2, real, at], joint[b // 2, imag, at] = now

    def sum_products(pairs):
        total = None
        for a, b in pairs:
            total = a * b if total is None else total + a * b
        return total

    def mix_conv(chunk):
        own = slice(chunk * HALF, (chunk + 1) * HALF)

        def tile_step(tile, _):
            real, imag, sign, ends = rows_of(tile)
            p_r = [spec[b, real, 0:HALF] for b in range(blocks)]
            p_i = [spec[b, imag, 0:HALF] for b in range(blocks)]
            h_r = [taps_spec[b, real, own] for b in range(blocks)]
            h_i = [taps_spec[b, imag, own] for b in range(blocks)]
            p_s = [p_r[b] + p_i[b] for b in range(blocks)]
            h_s = [h_r[b] + h_i[b] for b in range(blocks)]
            last = None
            for b in range(blocks):
                rr = sum_products((p_r[i], h_r[b - i]) for i in range(b + 1))
                ii = sum_products((p_i[i], h_i[b - i]) for i in range(b + 1))
                ss = sum_products((p_s[i], h_s[b - i]) for i in range(b + 1))
                now = (rr - jnp.where(ends, 0.0, ii), jnp.where(ends, ii, ss - rr - ii))
                put(b, real, imag, sign, now, last)
                last = now
            return 0

        lax.fori_loop(0, BLOCK // 8, tile_step, 0)

    def mix_grad():
        def tile_step(tile, _):
            real, imag, sign, ends = rows_of(tile)
            p_r = [spec[b, real, 0:HALF] for b in range(blocks)]
            p_i = [spec[b, imag, 0:HALF] for b in range(blocks)]
            g_r = [spec[b, real, HALF:lanes] for b in range(blocks)]
            g_i = [spec[b, imag, HALF:lanes] for b in range(blocks)]
            p_d = [p_r[b] - p_i[b] for b in range(blocks)]
            g_s = [g_r[b] + g_i[b] for b in range(blocks)]
            last = None
            for b in reversed(range(blocks)):
                rr = sum_products((p_r[i], g_r[b + i]) for i in range(blocks - b))
                ii = sum_products((p_i[i], g_i[b + i]) for i in range(blocks - b))
                ss = sum_products((p_d[i], g_s[b + i]) for i in range(blocks - b))
                now = (rr + jnp.where(ends, 0.0, ii), jnp.where(ends, ii, ss - rr + ii))
                put(b, real, imag, sign, now, last)
                last = now
            return 0

        lax.fori_loop(0, BLOCK // 8, tile_step, 0)

    def back(pair):
        value = joint[pair]
        high = value.astype(BF16)
        low = (value - high.astype(F32)).astype(BF16)
        return dot(inverse[0], high) + dot(inverse[0], low) + dot(inverse[1], high)

    def back_conv(chunk, send):
        own = slice(chunk * HALF, (chunk + 1) * HALF)

        def pair_step(index, _):
            pair = (z + index) % side
            result = back(pair)
            for part in range(4):
                target = 4 * pair + part
                value = result[(part % 2) * HALF : (part % 2 + 1) * HALF, (part // 2) * HALF : (part // 2 + 1) * HALF]
                product = incoming[chunk, target, :, 0:HALF].astype(F32)
                conv_own[chunk, target] = (value + skip[:, own] * product).astype(BF16)
            if send:

                @pl.when(index > 0)
                def _():
                    for part in range(4):
                        conv_copy(chunk, 4 * pair + part, ctx).start()
                    conv_copy(chunk, target_of(index), ctx).start()

            return 0

        lax.fori_loop(0, side, pair_step, 0)

    def back_grad(chunk):
        def pair_step(pair, _):
            result = back(pair)
            for part in range(4):
                value = result[(part % 2) * HALF : (part % 2 + 1) * HALF, (part // 2) * HALF : (part // 2 + 1) * HALF]
                grad[chunk, 4 * pair + part] = value * scale
            return 0

        lax.fori_loop(0, side, pair_step, 0)

    def reduce_copy(chunk, slot, source, target, device):
        return pltpu.make_async_remote_copy(
            src_ref=source, dst_ref=target, send_sem=red_send.at[chunk, slot],
            recv_sem=red_recv.at[chunk, slot], device_id={"dp": device},
        )

    def core_copy(chunk):
        return reduce_copy(chunk, 0, core_out.at[chunk], core_in.at[chunk], core_mate)

    def x_copy(chunk, i):
        device = ((x + i) % 4) * 4 + zh * 2 + core
        return reduce_copy(chunk, i, x_out.at[chunk, i - 1], x_in.at[chunk, i - 1], device)

    def z_copy(chunk):
        return reduce_copy(chunk, 4, z_out.at[chunk], z_in.at[chunk], z_mate)

    def core_stage(chunk):
        def part_step(index, _):
            core_out[chunk, index] = grad[chunk, 2 * index + 1 - core].astype(BF16)
            return 0

        lax.fori_loop(0, 8, part_step, 0)
        core_copy(chunk).start()

    def x_stage(chunk):
        core_copy(chunk).wait_recv()
        for i in (1, 2, 3):
            for half in (0, 1):
                j = 2 * ((x + i) % 4) + half
                x_out[chunk, i - 1, half] = (
                    grad[chunk, 2 * j + core] + core_in[chunk, j].astype(F32)
                ).astype(BF16)
            x_copy(chunk, i).start()

    def x_total(chunk, half):
        j = 2 * x + half
        total = grad[chunk, 2 * j + core] + core_in[chunk, j].astype(F32)
        for i in range(3):
            total = total + x_in[chunk, i, half].astype(F32)
        return total

    def z_stage(chunk):
        for i in (1, 2, 3):
            x_copy(chunk, i).wait_recv()
        z_out[chunk] = x_total(chunk, 1 - zh).astype(BF16)
        z_copy(chunk).start()

    def z_finish(chunk):
        z_copy(chunk).wait_recv()
        taps_grad[:, chunk * HALF : (chunk + 1) * HALF] = x_total(chunk, zh) + z_in[chunk].astype(F32)

    def first_transform(index, _):
        part_transform(0, index)
        return 0

    lax.fori_loop(0, blocks, first_transform, 0)
    mix_conv(0)
    back_conv(0, False)
    mix_grad()
    back_grad(0)
    core_stage(0)

    for far in (3, 2, 1, 0):

        def await_late(index, _):
            step = ranks - 1 - index
            late_copy(step, source_of(step)).wait_recv()
            if far:
                conv_copy(0, target_of(step), ctx).start()
            return 0

        lax.fori_loop((3 - far) * side, min((4 - far) * side, ranks - 1), await_late, 0)
        if far:
            conv_copy(0, target_of(far), ctx).start()
        from_z = (z + side - far) % side
        part_transform(1, 2 * from_z)
        part_transform(1, 2 * from_z + 1)
        if far == 3:
            x_stage(0)

    mix_conv(1)
    back_conv(1, True)
    z_stage(0)
    mix_grad()
    back_grad(1)
    core_stage(1)
    x_stage(1)

    def gate_part(chunk, source, value):
        cols = pl.ds(pl.multiple_of((source * 2 + chunk) * HALF, HALF), HALF)
        mixed[:, cols] = (gate[:, cols] * value.astype(F32)).astype(BF16)

    def gate_step(chunk):
        def one(index, _):
            step = ranks - 1 - index
            source = source_of(step)
            conv_copy(chunk, target_of(1), source).wait_recv()
            gate_part(chunk, source, conv_in[source, chunk])
            return 0

        return one

    z_stage(1)
    gate_part(0, ctx, conv_own[0, ctx])
    gate_part(1, ctx, conv_own[1, ctx])
    z_finish(0)
    halo_copy.wait_send()

    def drain_taps(step, _):
        taps_copy(dp, step, z_mate).wait_send()
        return 0

    lax.fori_loop(0, 15, drain_taps, 0)

    def drain_parts(step, _):
        body_copy(step, ctx).wait_send()
        head_copy(step, ctx).wait_send()
        late_copy(step, ctx).wait_send()
        return 0

    lax.fori_loop(1, ranks, drain_parts, 0)
    lax.fori_loop(0, ranks - 1, gate_step(0), 0)

    def drain_conv(chunk):
        def one(step, _):
            conv_copy(chunk, target_of(step), ctx).wait_send()
            return 0

        lax.fori_loop(1, ranks, one, 0)

    drain_conv(0)
    for chunk in range(2):
        core_copy(chunk).wait_send()
        for i in (1, 2, 3):
            x_copy(chunk, i).wait_send()
    z_copy(0).wait_send()
    lax.fori_loop(0, ranks - 1, gate_step(1), 0)
    drain_conv(1)
    z_finish(1)
    z_copy(1).wait_send()


def hand_over(mixed_in, grad_in, mixed, taps_grad, sems):
    stores = [
        pltpu.make_async_copy(mixed_in, mixed, sems.at[0]),
        pltpu.make_async_copy(grad_in, taps_grad, sems.at[1]),
    ]
    for store in stores:
        store.start()
    for store in stores:
        store.wait()


def per_device(projected, short_weight, filter_taps, skip_gain, upstream):
    rows, joined = projected.shape[1:]
    width = joined // 3
    ranks = 16
    lanes = 2 * HALF
    blocks = ranks * rows // BLOCK
    forward, inverse = (jnp.asarray(t) for t in make_tables())
    vmem = pl.BlockSpec(memory_space=pltpu.VMEM)
    anywhere = pl.BlockSpec(memory_space=pl.ANY)
    shapes = [
        jax.ShapeDtypeStruct((rows, width), BF16),
        jax.ShapeDtypeStruct((rows, lanes), F32),
    ]
    results = pl.pallas_call(
        functools.partial(kernel, WINDOW),
        out_shape=[pltpu.VMEM(shape.shape, shape.dtype) for shape in shapes],
        in_specs=[anywhere] * 7,
        out_specs=[vmem] * 2,
        scratch_shapes=[
            pltpu.VMEM((rows, joined), BF16),
            pltpu.VMEM((rows, width), BF16),
            pltpu.VMEM(short_weight.shape, F32),
            pltpu.VMEM((rows, lanes), F32),
            pltpu.VMEM((1, lanes), F32),
            pltpu.VMEM(forward.shape, BF16),
            pltpu.VMEM(inverse.shape, BF16),
            pltpu.VMEM((16, joined), BF16),
            pltpu.VMEM((16, joined // 8), F32),
            pltpu.VMEM((16, joined // 8), BF16),
            pltpu.VMEM((16, joined // 8), BF16),
            pltpu.VMEM((8, joined), F32),
            pltpu.VMEM((rows, width), F32),
            pltpu.VMEM((2, ranks, rows, lanes), BF16),
            pltpu.VMEM((2, ranks, rows, lanes), BF16),
            pltpu.VMEM((ranks, rows, lanes), BF16),
            pltpu.VMEM((blocks, 2 * BLOCK, lanes), F32),
            pltpu.VMEM((blocks, 2 * BLOCK, lanes), F32),
            pltpu.VMEM((blocks // 2, 2 * BLOCK, lanes), F32),
            pltpu.VMEM((2, ranks, rows, HALF), BF16),
            pltpu.VMEM((ranks, 2, rows, HALF), BF16),
            pltpu.VMEM((2, ranks, rows, HALF), F32),
            pltpu.VMEM((2, 8, rows, HALF), BF16),
            pltpu.VMEM((2, 8, rows, HALF), BF16),
            pltpu.VMEM((2, 3, 2, rows, HALF), BF16),
            pltpu.VMEM((2, 3, 2, rows, HALF), BF16),
            pltpu.VMEM((2, rows, HALF), BF16),
            pltpu.VMEM((2, rows, HALF), BF16),
            pltpu.SemaphoreType.DMA((4, 4)),
            pltpu.SemaphoreType.DMA((6,)),
            pltpu.SemaphoreType.DMA((2,)),
            pltpu.SemaphoreType.DMA((16,)),
            pltpu.SemaphoreType.DMA((16,)),
            pltpu.SemaphoreType.DMA((16,)),
            pltpu.SemaphoreType.DMA((16,)),
            pltpu.SemaphoreType.DMA((2, 16)),
            pltpu.SemaphoreType.DMA((2, 16)),
            pltpu.SemaphoreType.DMA((2, 16)),
            pltpu.SemaphoreType.DMA((16, 2)),
            pltpu.SemaphoreType.DMA((2, 5)),
            pltpu.SemaphoreType.DMA((2, 5)),
        ],
        compiler_params=pltpu.CompilerParams(
            collective_id=0, has_side_effects=True, vmem_limit_bytes=60 * 2**20
        ),
    )(
        projected.reshape(rows, joined), short_weight, filter_taps, skip_gain.reshape(1, lanes),
        upstream.reshape(rows, width), forward, inverse,
    )
    mixed, taps_grad = pl.pallas_call(
        hand_over,
        out_shape=shapes,
        in_specs=[vmem] * 2,
        out_specs=[anywhere] * 2,
        scratch_shapes=[pltpu.SemaphoreType.DMA((2,))],
        compiler_params=pltpu.CompilerParams(vmem_limit_bytes=4 * 2**20),
    )(*results)
    return (mixed.reshape(1, rows, width), taps_grad)


def solution(mesh):
    in_specs = (P("dp", "ctx", None), P(), P("dp", "ctx"), P("ctx"), P("dp", "ctx", None))
    out_specs = (P("dp", "ctx", None), P("dp", "ctx"))
    return jax.shard_map(
        per_device, mesh=mesh, in_specs=in_specs, out_specs=out_specs, check_vma=False
    )
```
